512 devices in a mesh: attn: 8 (over y, core), expert: 16 (over z), tp: 4 (over x).
Axes of the slice: x: 4, y: 4, z: 16, core: 2. Of those that a mesh axis runs over, the one named last changes fastest.
Arguments:
- query: bfloat16 [2048, 8192], P(('attn', 'expert'), 'tp'), may hold values from -9 to 9
- cached_key_store: bfloat16 [2048, 128, 512], P(('attn', 'expert'), None, 'tp'), may hold values from -5 to 5
- cached_value_store: bfloat16 [2048, 128, 512], P(('attn', 'expert'), None, 'tp'), may hold values from -5 to 5
- token_keys: bfloat16 [2048, 512], P(('attn', 'expert'), 'tp'), may hold values from -5 to 5
- token_values: bfloat16 [2048, 512], P(('attn', 'expert'), 'tp'), may hold values from -5 to 5
- lengths: int32 [2048], P(('attn', 'expert')), may hold values from 2 to 128, as said below
- out_weight: bfloat16 [8192, 2048], P('tp', 'expert'), may hold values from -0.25 to 0.25
- resid: bfloat16 [2048, 2048], P(('attn', 'expert', 'tp')), may hold values from -300 to 300
- norm_gain: float32 [2048], replicated, may hold values from 0.1 to 1.9
- routes: int32 [2048, 8], P(('attn', 'expert')), may hold values from 0 to 127, all different within a row; in each aligned block of 16 rows (0 to 15, 16 to 31, ...) at most 2 rows name the same one
- route_weight: float32 [2048, 8], P(('attn', 'expert')), may hold values from 0.02 to 0.3
- w_gate: bfloat16 [128, 2048, 768], P(('attn', 'expert'), None, 'tp'), may hold values from -0.125 to 0.125
- w_up: bfloat16 [128, 2048, 768], P(('attn', 'expert'), None, 'tp'), may hold values from -0.125 to 0.125
- w_down: bfloat16 [128, 768, 2048], P(('attn', 'expert'), 'tp'), may hold values from -0.4375 to 0.4375
Outputs:
- mixed: bfloat16 [2048, 2048], P(('attn', 'expert', 'tp'))
The draws below stay inside these ranges and needn't reach their ends.
Inputs may be any that keep to these rules, and one draw needn't show every extreme that they name: `routes`: in each aligned block of 16 rows no expert is named by more than 2 rows, a bound that some block reaches. `lengths`: every aligned block of 16 rows holds a row with exactly 128.
All inputs are finite; a program needn't handle non-finite values.
Results may differ from the reference program's by a relative error of at most 0.012.
Values may be sent and summed in bfloat16 or wider, within the bound.
No kernel may reach another device: no remote copies, remote signals or barrier semaphores. Data moves between devices by JAX's collectives and lax.ppermute only.
A program may use at most 64 MiB of HBM per device.

```python
import math
import jax
import jax.numpy as jnp
import numpy as np
from jax import lax

D = 2048
QUERY_HEADS = 64
KEY_VALUE_HEADS = 4
HEAD_SIZE = 128
FF = 768
TOPK = 8
GROUP_ROWS = 16
CACHE_POSITIONS = 128
EXPERTS = 128
BATCH_ROWS = 2048
CAP = 2
N_TP = 4


def draw_query(key, part):
    key = jax.random.fold_in(key, 21)
    value_entries = jnp.clip(jax.random.normal(key, (BATCH_ROWS, QUERY_HEADS * HEAD_SIZE), jnp.float32), -5.0, 5.0)
    return value_entries.astype(jnp.bfloat16)


def draw_cached_key_store(key, part):
    key = jax.random.fold_in(key, 22)
    value_entries = jnp.clip(jax.random.normal(key, (BATCH_ROWS, CACHE_POSITIONS, KEY_VALUE_HEADS * HEAD_SIZE), jnp.float32), -5.0, 5.0)
    return value_entries.astype(jnp.bfloat16)


def draw_resid(key, part):
    key = jax.random.fold_in(key, 31)
    value_entries = jnp.clip(jax.random.normal(jax.random.fold_in(key, 1), (BATCH_ROWS, D), jnp.float32), -3.0, 3.0)
    return value_entries.astype(jnp.bfloat16)


def draw_lengths(key, part):
    key = jax.random.fold_in(key, 41)
    blocks = BATCH_ROWS // GROUP_ROWS
    drawn = jax.random.randint(jax.random.fold_in(key, 1), (BATCH_ROWS,), 2, CACHE_POSITIONS + 1)
    chosen = jax.random.randint(jax.random.fold_in(key, 2), (blocks,), 0, GROUP_ROWS)
    marked = jnp.arange(BATCH_ROWS, dtype=jnp.int32) % GROUP_ROWS == jnp.repeat(chosen, GROUP_ROWS)
    return jnp.where(marked, CACHE_POSITIONS, drawn).astype(jnp.int32)


def level_of(key, dims, shards, least, high):
    gain, own = 1.0, jax.random.fold_in(key, 6)
    for dim, blocks in shards:
        steps = jnp.exp(jax.random.uniform(jax.random.fold_in(own, dim), (blocks,), jnp.float32, least / len(shards), high / len(shards)))
        gain = gain * jnp.repeat(steps, dims[dim] // blocks).reshape([-1 if axis == dim else 1 for axis in range(len(dims))])
    return gain


def routed_block(own_key, own, number, rows, amount, top, limit, skew):
    ranking = jax.random.permutation(own_key, amount)
    crowded, common = load_shares(amount, rows * top, limit, skew, True), load_shares(amount, rows * top, limit, skew, False)
    places = jnp.arange(amount)

    def named(tallies, offset_by):
        used = int((tallies > 0).sum())
        fixed = max(1, used // 4)
        passed = fixed + (places - fixed + offset_by * (used - fixed)) % max(1, amount - fixed)
        return jnp.zeros((amount,), jnp.int32).at[ranking[jnp.where(places < fixed, places, passed)]].set(jnp.asarray(tallies, jnp.int32))

    tallies = jnp.where(number % 4 == 0, named(crowded, number // 4), named(common, number - number // 4 - 1))
    mixed = jax.random.permutation(jax.random.fold_in(own, 3), amount)
    giver, taker = mixed[0:amount // 2 * 2:2], mixed[1:amount // 2 * 2:2]
    slack = jnp.minimum(tallies[giver] - 1, limit - tallies[taker]) // 2
    slack = jnp.where((giver == ranking[0]) | (taker == ranking[0]) | (tallies[taker] == 0), 0, jnp.maximum(slack, 0))
    passed = jax.random.randint(jax.random.fold_in(own, 4), (amount // 2,), 0, 1 << 20) % (slack + 1)
    tallies = tallies.at[giver].add(-passed).at[taker].add(passed)
    members = jnp.searchsorted(jnp.cumsum(tallies), jnp.arange(rows * top), side="right").astype(jnp.int32)
    table = members.reshape(top, rows).T
    table = table[jax.random.permutation(jax.random.fold_in(own, 1), rows)]
    offset_by = jax.random.randint(jax.random.fold_in(own, 2), (rows, 1), 0, top)
    return jnp.take_along_axis(table, (jnp.arange(top)[None, :] + offset_by) % top, axis=1)


def load_shares(number_of, total, most, skew, full):
    weights = [(1 << 20) // math.isqrt(standing ** skew) + 1 for standing in range(1, number_of + 1)]
    largest = most if full else min(most, max(-(-total // number_of), total * weights[0] // sum(weights)))
    least = 1 if total - largest >= number_of - 1 else 0
    given, rest = [largest] + [least] * (number_of - 1), total - largest - least * (number_of - 1)
    while rest > 0:
        candidates = [i for i in range(1, number_of) if given[i] < largest] or [i for i in range(1, number_of) if given[i] < most]
        pool, budget = sum([weights[i] for i in candidates]), rest
        for i in candidates:
            more = min(most - given[i], max(1, budget * weights[i] // pool), rest)
            given[i] = given[i] + more
            rest = rest - more
    return np.array(given)


def centred(stream_key, extent, scale, limit, split=(), kind=jnp.bfloat16):
    factor_of = level_of(stream_key, extent, split, -0.22, 0.18) if split else 1.0
    values = jax.random.normal(stream_key, extent, jnp.float32) * scale * factor_of
    return jnp.minimum(jnp.maximum(values, -limit), limit).astype(kind)


def setup_inputs(seed: int = 0) -> dict:
    key_list = jax.random.split(jax.random.key(seed), 15)
    query = draw_query(jax.random.fold_in(key_list[14], 71), 0)
    cached_key_store = draw_cached_key_store(jax.random.fold_in(key_list[14], 71), 0)
    cached_value_store = centred(key_list[2], (BATCH_ROWS, CACHE_POSITIONS, KEY_VALUE_HEADS * HEAD_SIZE), 1.0, 5.0, ((0, 128), (2, 4)))
    token_keys = centred(key_list[3], (BATCH_ROWS, KEY_VALUE_HEADS * HEAD_SIZE), 1.0, 5.0, ((0, 128), (1, 4)))
    token_values = centred(key_list[4], (BATCH_ROWS, KEY_VALUE_HEADS * HEAD_SIZE), 1.0, 5.0, ((0, 128), (1, 4)))
    lengths = draw_lengths(jax.random.fold_in(key_list[14], 71), 0)
    out_weight = centred(key_list[6], (QUERY_HEADS * HEAD_SIZE, D), (QUERY_HEADS * HEAD_SIZE // 16) ** -0.5, 0.25, ((0, 4), (1, 16)))
    resid = draw_resid(jax.random.fold_in(key_list[14], 71), 0)
    norm_gain = jnp.clip(1.0 + 0.18 * jax.random.normal(key_list[8], (D,), jnp.float32), 0.1, 1.9)
    routes_keys = jax.random.split(jax.random.fold_in(key_list[9], 1), BATCH_ROWS // GROUP_ROWS)
    routes_turns = jax.random.permutation(jax.random.fold_in(key_list[9], 3), BATCH_ROWS // GROUP_ROWS)
    routes = jax.vmap(lambda own, number: routed_block(jax.random.fold_in(key_list[9], 2), own, number, GROUP_ROWS, EXPERTS, TOPK, CAP, 2))(routes_keys, routes_turns).reshape((BATCH_ROWS, TOPK))
    route_weight = jnp.clip(0.02 + 0.28 * jax.random.uniform(key_list[10], (BATCH_ROWS, TOPK), jnp.float32) ** level_of(key_list[10], (BATCH_ROWS, TOPK), ((0, 128),), -0.2, 0.2), 0.02, 0.3)
    w_gate = centred(key_list[11], (EXPERTS, D, FF), D ** -0.5, 0.125, ((0, 128), (2, 4)))
    w_up = centred(key_list[12], (EXPERTS, D, FF), D ** -0.5, 0.125, ((0, 128), (2, 4)))
    w_down = centred(key_list[13], (EXPERTS, FF, D), (FF // 4) ** -0.5, 0.4375, ((0, 128), (1, 4)))
    return dict(query=query, cached_key_store=cached_key_store, cached_value_store=cached_value_store, token_keys=token_keys, token_values=token_values, lengths=lengths, out_weight=out_weight, resid=resid, norm_gain=norm_gain, routes=routes, route_weight=route_weight, w_gate=w_gate, w_up=w_up, w_down=w_down)


def normalize(hidden_state, norm_gain):
    square_mean = lax.optimization_barrier(jnp.mean(hidden_state * hidden_state, axis=-1, keepdims=True))
    return (hidden_state * lax.rsqrt(square_mean + 1e-06) * norm_gain.astype(jnp.float32)).astype(jnp.bfloat16)

def reference(query, cached_key_store, cached_value_store, token_keys, token_values, lengths, out_weight, resid, norm_gain, routes, route_weight, w_gate, w_up, w_down):
    query_group_size = QUERY_HEADS // KEY_VALUE_HEADS
    score_scale = 1.0 / math.sqrt(HEAD_SIZE)
    query_rows = query.astype(jnp.float32).reshape(BATCH_ROWS, KEY_VALUE_HEADS, query_group_size, HEAD_SIZE)
    key_row_list = cached_key_store.astype(jnp.float32).reshape(BATCH_ROWS, CACHE_POSITIONS, KEY_VALUE_HEADS, HEAD_SIZE)
    value_row_list = cached_value_store.astype(jnp.float32).reshape(BATCH_ROWS, CACHE_POSITIONS, KEY_VALUE_HEADS, HEAD_SIZE)
    incoming_key = token_keys.astype(jnp.float32).reshape(BATCH_ROWS, KEY_VALUE_HEADS, HEAD_SIZE)
    incoming_value = token_values.astype(jnp.float32).reshape(BATCH_ROWS, KEY_VALUE_HEADS, HEAD_SIZE)
    scores = jnp.einsum('rkgd,rjkd->rkgj', query_rows, key_row_list, precision=lax.Precision.HIGHEST) * score_scale
    fresh_score = jnp.einsum('rkgd,rkd->rkg', query_rows, incoming_key, precision=lax.Precision.HIGHEST) * score_scale
    valid = (jnp.arange(CACHE_POSITIONS, dtype=jnp.int32)[None, :] < lengths[:, None])[:, None, None, :]
    masked = jnp.where(valid, scores, -jnp.inf)
    row_max = jnp.maximum(lax.optimization_barrier(jnp.max(masked, axis=-1)), fresh_score)
    expo = jnp.where(valid, jnp.exp(masked - row_max[..., None]), 0.0)
    fresh_expo = jnp.exp(fresh_score - row_max)
    denominator = lax.optimization_barrier(jnp.sum(expo, axis=-1)) + fresh_expo
    weights_cache = (expo / denominator[..., None]).astype(jnp.bfloat16)
    weights_fresh = (fresh_expo / denominator).astype(jnp.bfloat16)
    attn_mixed = jnp.einsum('rkgj,rjkd->rkgd', weights_cache.astype(jnp.float32), value_row_list, precision=lax.Precision.HIGHEST)
    attn_mixed = attn_mixed + weights_fresh.astype(jnp.float32)[..., None] * incoming_value[:, :, None, :]
    attended = attn_mixed.reshape(BATCH_ROWS, QUERY_HEADS * HEAD_SIZE).astype(jnp.bfloat16)
    hidden_state = resid.astype(jnp.float32) + jnp.dot(attended, out_weight, preferred_element_type=jnp.float32)
    normed = normalize(hidden_state, norm_gain)
    blocks = BATCH_ROWS // GROUP_ROWS
    pick_ids = routes.reshape(blocks, GROUP_ROWS * TOPK)
    hot_table = (pick_ids[..., None] == jnp.arange(EXPERTS, dtype=jnp.int32)[None, None, :]).astype(jnp.int32)
    before = jnp.cumsum(hot_table, axis=1) - hot_table
    slot_rank = lax.optimization_barrier(jnp.sum(before * hot_table, axis=-1)).astype(jnp.int32)
    slot_index = (jnp.arange(blocks, dtype=jnp.int32)[:, None] * CAP + slot_rank).reshape(-1)
    expert_of = pick_ids.reshape(-1)
    source_rows = jnp.repeat(normed, TOPK, axis=0)
    buffer = jnp.zeros((EXPERTS, blocks * CAP, D), jnp.bfloat16).at[expert_of, slot_index].set(source_rows)
    block_width = FF // N_TP

    def expert_rows(pack):
        tokens_in, gate_matrix, up_matrix, down_matrix = pack
        gate_value = jnp.dot(tokens_in, gate_matrix, preferred_element_type=jnp.float32)
        up_value = jnp.dot(tokens_in, up_matrix, preferred_element_type=jnp.float32)
        activated = (jax.nn.silu(gate_value) * up_value).astype(jnp.bfloat16)
        pieces = jnp.einsum('sbf,bfd->sbd', activated.reshape(-1, N_TP, block_width).astype(jnp.float32), down_matrix.reshape(N_TP, block_width, D).astype(jnp.float32), precision=lax.Precision.HIGHEST)
        rounded = lax.optimization_barrier(pieces.astype(jnp.bfloat16))
        return lax.optimization_barrier(jnp.sum(rounded.astype(jnp.float32), axis=1))
    produced = lax.map(expert_rows, (buffer, w_gate, w_up, w_down))
    picked = produced[expert_of, slot_index].reshape(BATCH_ROWS, TOPK, D)
    expert_sum = lax.optimization_barrier(jnp.sum(picked * route_weight[:, :, None], axis=1))
    return (hidden_state + expert_sum).astype(jnp.bfloat16)
```

```python
import math

import jax
import jax.numpy as jnp
from jax import lax
from jax.experimental import pallas as pl
from jax.experimental.pallas import tpu as pltpu
from jax.sharding import Mesh
from jax.sharding import PartitionSpec as P

HEADS = 16
HEAD_SIZE = 128
POSITIONS = 128
ROWS = 16
ATTN = 8
Z_HI = 4
Z_LO = 4
EXPERT = Z_HI * Z_LO
TP = 4
D = 2048
LANES = 128
QUARTER = D // TP
SLOTS = 32
FF = 192
TOPK = 8
BF16 = jnp.bfloat16
F32 = jnp.float32

VMEM = pl.BlockSpec(memory_space=pltpu.VMEM)
SMEM = pl.BlockSpec(memory_space=pltpu.SMEM)
PARAMS = pltpu.CompilerParams(vmem_limit_bytes=40 * 1024 * 1024)


def call(kernel, outs, in_specs, scratch=()):
    shapes = [jax.ShapeDtypeStruct(s, d) for s, d in outs]
    single = len(shapes) == 1
    return pl.pallas_call(
        kernel,
        out_shape=shapes[0] if single else shapes,
        in_specs=in_specs,
        out_specs=VMEM if single else [VMEM] * len(shapes),
        scratch_shapes=list(scratch),
        compiler_params=PARAMS,
    )


def attention_kernel(place, lengths, query, keys, values, new_keys, new_values, resid, meta, out, q_rows, a_rows, extra):
    for h in range(HEADS):
        q_rows[:, h, :] = query[:, h * HEAD_SIZE : (h + 1) * HEAD_SIZE].astype(F32)
    scale = 1.0 / math.sqrt(HEAD_SIZE)
    position = lax.broadcasted_iota(jnp.int32, (HEADS, POSITIONS), 1)
    new_k = new_keys[...].astype(F32)
    new_v = new_values[...].astype(F32)
    for r in range(ROWS):
        q = q_rows[r]
        scores = lax.dot_general(
            q.astype(BF16), keys[r], (((1,), (1,)), ((), ())), preferred_element_type=F32
        ) * scale
        fresh = jnp.sum(q * new_k[r : r + 1, :], axis=1, keepdims=True) * scale
        valid = position < lengths[r]
        top = jnp.maximum(jnp.max(jnp.where(valid, scores, -jnp.inf), axis=1, keepdims=True), fresh)
        expo = jnp.where(valid, jnp.exp(scores - top), 0.0)
        fresh_expo = jnp.exp(fresh - top)
        total = jnp.sum(expo, axis=1, keepdims=True) + fresh_expo
        weights = (expo / total).astype(BF16)
        fresh_weight = (fresh_expo / total).astype(BF16).astype(F32)
        mixed = jnp.dot(weights, values[r], preferred_element_type=F32)
        a_rows[:, r, :] = mixed + fresh_weight * new_v[r : r + 1, :]
    tp = place[2]
    extra[...] = jnp.zeros_like(extra)
    for e in range(EXPERT):
        extra[e, pl.ds(tp * 4, 4), :] = resid[:, e * LANES : (e + 1) * LANES].astype(F32)
        extra[e, pl.ds(lax.rem(tp + 1, 4) * 4, 4), :] = meta[...]
    for lo in range(Z_LO):
        heads = a_rows[4 * lo : 4 * lo + 4].astype(BF16).reshape(4 * ROWS, HEAD_SIZE)
        for hi in range(Z_HI):
            out[hi * Z_LO + lo, 0 : 4 * ROWS, :] = heads
    out[:, 4 * ROWS : 5 * ROWS, :] = extra[...].astype(BF16)


def project_kernel(place, gathered, weight, out):
    heads = [gathered[:, h * ROWS : (h + 1) * ROWS, :].reshape(EXPERT * ROWS, HEAD_SIZE) for h in range(4)]
    rows = jnp.concatenate(heads, axis=1)
    lo, tp = place[1], place[2]
    extra = gathered[:, 4 * ROWS : 5 * ROWS, :].astype(F32)
    line = lax.broadcasted_iota(jnp.int32, extra.shape, 1)
    resid = jnp.where((line >= tp * 4) & (line < tp * 4 + 4), extra, 0.0).reshape(EXPERT * ROWS, LANES)
    for j in range(TP):
        part = jnp.dot(rows, weight[j], preferred_element_type=F32)
        part = part + jnp.where(lo == j, resid, 0.0)
        part = part.astype(BF16)
        for i in range(Z_LO):
            out[i * TP + j] = part[i * 64 : (i + 1) * 64, :]


def reduce_kernel(parts, out):
    total = parts[0].astype(F32)
    for i in range(1, Z_LO * TP):
        total = total + parts[i].astype(F32)
    total = total.astype(BF16)
    for i in range(EXPERT):
        out[i] = total


def select_kernel(place, gathered, hidden, out, combine):
    tp = place[2]
    mine = place[0] * Z_LO + place[1]
    extra = gathered[:, 4 * ROWS : 5 * ROWS, :].astype(F32)
    line = lax.broadcasted_iota(jnp.int32, extra.shape, 1)
    base = lax.rem(tp + 1, 4) * 4
    route = jnp.sum(jnp.where(line == base, extra, 0.0), axis=1)
    high = jnp.sum(jnp.where(line == base + 1, extra, 0.0), axis=1)
    low = jnp.sum(jnp.where(line == base + 2, extra, 0.0), axis=1)
    pick_row = lax.broadcasted_iota(jnp.int32, (LANES, EXPERT * ROWS), 0) // TOPK
    row = lax.rem(lax.broadcasted_iota(jnp.int32, (LANES, EXPERT * ROWS), 1), ROWS)
    here = jnp.where(pick_row == row, 1.0, 0.0).astype(BF16)
    earlier = jnp.where(pick_row < row, 1.0, 0.0).astype(BF16)
    hits = [jnp.where(route == (a * EXPERT + mine).astype(F32), 1.0, 0.0) for a in range(ATTN)]
    hit = jnp.concatenate(hits, axis=0)
    hit_high = jnp.concatenate([m * high for m in hits], axis=0)
    hit_low = jnp.concatenate([m * low for m in hits], axis=0)
    shape = (ATTN * EXPERT, EXPERT * ROWS)
    own = lax.rem(lax.broadcasted_iota(jnp.int32, shape, 0), EXPERT) == (
        lax.broadcasted_iota(jnp.int32, shape, 1) // ROWS
    )
    dot = lambda a, b: jnp.dot(a.astype(BF16), b, preferred_element_type=F32)
    named = jnp.where(own, dot(hit, here), 0.0)
    rank = dot(hit, earlier)
    weight_high = dot(hit_high, here)
    weight_low = dot(hit_low, here)
    chosen = [jnp.where(rank == s, named, 0.0) for s in (0.0, 1.0)]

    def laid(pair):
        return jnp.concatenate(
            [pair[s][a * EXPERT : (a + 1) * EXPERT, :] for a in range(ATTN) for s in range(2)], axis=0
        )

    choice = laid(chosen).astype(BF16)
    combine[0] = jnp.transpose(laid([c * weight_high for c in chosen])).astype(BF16)
    combine[1] = jnp.transpose(laid([c * weight_low for c in chosen])).astype(BF16)
    for hi in range(Z_HI):
        block = hidden[hi * Z_LO : (hi + 1) * Z_LO].reshape(EXPERT * ROWS, LANES)
        sent = jnp.dot(choice, block, preferred_element_type=F32).astype(BF16)
        sent = sent.reshape(ATTN, SLOTS, LANES)
        for t in range(TP):
            out[:, t, :, hi * LANES : (hi + 1) * LANES] = sent


def expert_kernel(tokens, gain, w_gate, w_up, w_down, out, x, normed):
    slots = ATTN * SLOTS
    square = jnp.zeros((slots, LANES), F32)
    for hi in range(Z_HI):
        for t in range(TP):
            c = hi * TP + t
            block = tokens[:, t, :, hi * LANES : (hi + 1) * LANES].reshape(slots, LANES).astype(F32)
            x[:, c * LANES : (c + 1) * LANES] = block
            square = square + block * block
    factor = lax.rsqrt(jnp.sum(square, axis=1, keepdims=True) * (1.0 / D) + 1e-06)
    normed[...] = (x[...] * factor * gain[...]).astype(BF16)
    gate = jnp.dot(normed[...], w_gate[...], preferred_element_type=F32)
    up = jnp.dot(normed[...], w_up[...], preferred_element_type=F32)
    activated = (gate / (1.0 + jnp.exp(-gate)) * up).astype(BF16)
    for hi in range(Z_HI):
        for t in range(TP):
            c = hi * TP + t
            part = jnp.dot(activated, w_down[:, c * LANES : (c + 1) * LANES], preferred_element_type=F32)
            out[:, t, :, hi * LANES : (hi + 1) * LANES] = part.astype(BF16).reshape(ATTN, SLOTS, LANES)


def combine_kernel(parts, combine, out):
    total = jnp.zeros((EXPERT * ROWS, QUARTER), F32)
    for t in range(TP):
        block = parts[:, t].reshape(ATTN * SLOTS, QUARTER)
        total = total + jnp.dot(combine[0], block, preferred_element_type=F32)
        total = total + jnp.dot(combine[1], block, preferred_element_type=F32)
    out[...] = total.astype(BF16).reshape(EXPERT, ROWS, QUARTER)


def exchange(x, axes):
    return lax.all_to_all(x, axes, split_axis=0, concat_axis=0, tiled=True)


def shards(
    query,
    cached_key_store,
    cached_value_store,
    token_keys,
    token_values,
    lengths,
    out_weight,
    resid,
    norm_gain,
    routes,
    route_weight,
    w_gate,
    w_up,
    w_down,
):
    z = ("zhi", "zlo")
    z_hi, z_lo, tp = (lax.axis_index(n) for n in ("zhi", "zlo", "tp"))
    place = jnp.stack([z_hi, z_lo, tp]).astype(jnp.int32)
    high = route_weight.astype(BF16).astype(F32)
    meta = jnp.stack(
        [v.reshape(LANES) for v in (routes.astype(F32), high, route_weight - high, jnp.zeros_like(high))]
    )
    weight = exchange(out_weight.reshape(Z_LO, D // Z_LO, LANES), "zlo")
    sent = call(
        attention_kernel,
        [((EXPERT, 5 * ROWS, LANES), BF16)],
        [SMEM, SMEM] + [VMEM] * 7,
        [
            pltpu.VMEM((ROWS, HEADS, HEAD_SIZE), F32),
            pltpu.VMEM((HEADS, ROWS, HEAD_SIZE), F32),
            pltpu.VMEM((EXPERT, ROWS, LANES), F32),
        ],
    )(place, lengths, query, cached_key_store, cached_value_store, token_keys, token_values, resid, meta)
    gathered = exchange(sent, z)
    parts = call(project_kernel, [((Z_LO * TP, 64, LANES), BF16)], [SMEM, VMEM, VMEM])(place, gathered, weight)
    parts = exchange(parts, ("zlo", "tp"))
    own = call(reduce_kernel, [((EXPERT, 64, LANES), BF16)], [VMEM])(parts)
    hidden = exchange(own, z)
    outgoing, combine = call(
        select_kernel,
        [((ATTN, TP, SLOTS, QUARTER), BF16), ((2, EXPERT * ROWS, ATTN * SLOTS), BF16)],
        [SMEM, VMEM, VMEM],
    )(place, gathered, hidden)
    incoming = exchange(outgoing.reshape(ATTN * TP, SLOTS, QUARTER), ("attn", "tp"))
    produced = call(
        expert_kernel,
        [((ATTN, TP, SLOTS, QUARTER), BF16)],
        [VMEM] * 5,
        [pltpu.VMEM((ATTN * SLOTS, D), F32), pltpu.VMEM((ATTN * SLOTS, D), BF16)],
    )(incoming.reshape(ATTN, TP, SLOTS, QUARTER), norm_gain.reshape(1, D), w_gate[0], w_up[0], w_down[0])
    returned = exchange(produced.reshape(ATTN * TP, SLOTS, QUARTER), ("attn", "tp"))
    weighted = call(combine_kernel, [((EXPERT, ROWS, QUARTER), BF16)], [VMEM, VMEM])(
        returned.reshape(ATTN, TP, SLOTS, QUARTER), combine
    )
    back = exchange(weighted, z)
    own_hidden = lax.dynamic_slice_in_dim(
        hidden.reshape(Z_HI, EXPERT, ROWS, LANES), z_hi * Z_LO + z_lo, 1, axis=1
    )[:, 0]
    own_hidden = own_hidden.transpose(1, 0, 2).reshape(ROWS, QUARTER).astype(F32)
    mixed = (jnp.sum(back.astype(F32), axis=0) + own_hidden).astype(BF16)
    mine = exchange(mixed.reshape(TP, ROWS // TP, QUARTER), "tp")
    return mine.reshape(TP, ROWS // TP, Z_HI, LANES).transpose(1, 2, 0, 3).reshape(ROWS // TP, D)


def solution(mesh):
    fine = Mesh(mesh.devices.reshape(ATTN, Z_HI, Z_LO, TP), ("attn", "zhi", "zlo", "tp"))
    rows = ("attn", "zhi", "zlo")
    in_specs = (
        P(rows, "tp"),
        P(rows, None, "tp"),
        P(rows, None, "tp"),
        P(rows, "tp"),
        P(rows, "tp"),
        P(rows),
        P("tp", ("zhi", "zlo")),
        P((*rows, "tp"), None),
        P(),
        P(rows, None),
        P(rows, None),
        P(rows, None, "tp"),
        P(rows, None, "tp"),
        P(rows, "tp", None),
    )
    out_specs = P((*rows, "tp"), None)
    return jax.shard_map(shards, mesh=fine, in_specs=in_specs, out_specs=out_specs, check_vma=False)
```

```python
import math

import jax
import jax.numpy as jnp
from jax import lax
from jax.experimental import pallas as pl
from jax.experimental.pallas import tpu as pltpu
from jax.sharding import Mesh
from jax.sharding import PartitionSpec as P

HEADS = 16
HEAD_SIZE = 128
POSITIONS = 128
ROWS = 16
ATTN = 8
Z_HI = 4
Z_LO = 4
EXPERT = Z_HI * Z_LO
TP = 4
D = 2048
LANES = 128
QUARTER = D // TP
SLOTS = 32
FF = 192
TOPK = 8
PIECES = 4
BF16 = jnp.bfloat16
F32 = jnp.float32

VMEM = pl.BlockSpec(memory_space=pltpu.VMEM)
SMEM = pl.BlockSpec(memory_space=pltpu.SMEM)
ANY = pl.BlockSpec(memory_space=pl.ANY)
PARAMS = pltpu.CompilerParams(vmem_limit_bytes=40 * 1024 * 1024)


def call(kernel, outs, in_specs, scratch=(), megabytes=4):
    shapes = [jax.ShapeDtypeStruct(s, d) for s, d in outs]
    single = len(shapes) == 1
    return pl.pallas_call(
        kernel,
        out_shape=shapes[0] if single else shapes,
        in_specs=in_specs,
        out_specs=VMEM if single else [VMEM] * len(shapes),
        scratch_shapes=list(scratch),
        compiler_params=PARAMS,
        cost_estimate=pl.CostEstimate(flops=0, bytes_accessed=megabytes << 20, transcendentals=0),
    )


def attention_kernel(
    place, lengths, query, keys_hbm, values_hbm, new_keys, new_values, resid, routes, route_weight, out,
    keys, values, q_rows, a_rows, extra, sems,
):
    share = ROWS // PIECES
    copies = []
    for n, (source, target) in enumerate(((keys_hbm, keys), (values_hbm, values))):
        for c in range(PIECES):
            part = pl.ds(c * share, share)
            copies.append(pltpu.make_async_copy(source.at[part], target.at[part], sems.at[n * PIECES + c]))
            copies[-1].start()
    tp = place[2]
    high = route_weight[...].astype(BF16)
    low = (route_weight[...] - high.astype(F32)).astype(BF16)
    pick = lax.rem(lax.broadcasted_iota(jnp.int32, (TOPK, LANES), 1), TOPK)
    spread = jnp.where(pick == lax.broadcasted_iota(jnp.int32, (TOPK, LANES), 0), 1.0, 0.0).astype(BF16)
    diagonal = lax.broadcasted_iota(jnp.int32, (ROWS, LANES), 1) // TOPK == lax.broadcasted_iota(
        jnp.int32, (ROWS, LANES), 0
    )
    extra[...] = jnp.zeros_like(extra)
    for n, table in enumerate((routes[...].astype(F32).astype(BF16), high, low)):
        wide = jnp.dot(table, spread, preferred_element_type=F32)
        line = jnp.sum(jnp.where(diagonal, wide, 0.0), axis=0, keepdims=True)
        for e in range(EXPERT):
            extra[e, pl.ds(lax.rem(tp + 1, 4) * 4 + n, 1), :] = line
    for e in range(EXPERT):
        extra[e, pl.ds(tp * 4, 4), :] = resid[:, e * LANES : (e + 1) * LANES].astype(F32)
    out[:, 4 * ROWS : 5 * ROWS, :] = extra[...].astype(BF16)
    for h in range(HEADS):
        q_rows[:, h, :] = query[:, h * HEAD_SIZE : (h + 1) * HEAD_SIZE].astype(F32)
    scale = 1.0 / math.sqrt(HEAD_SIZE)
    position = lax.broadcasted_iota(jnp.int32, (HEADS, POSITIONS), 1)
    scores = []
    for r in range(ROWS):
        if r % share == 0:
            copies[r // share].wait()
        product = lax.dot_general(
            q_rows[r].astype(BF16), keys[r], (((1,), (1,)), ((), ())), preferred_element_type=F32
        )
        scores.append(jnp.where(position < lengths[r], product * scale, -jnp.inf))
    scores = jnp.stack(scores)
    fresh = jnp.sum(q_rows[...] * new_keys[...].astype(F32)[:, None, :], axis=2, keepdims=True) * scale
    top = jnp.maximum(jnp.max(scores, axis=2, keepdims=True), fresh)
    expo = jnp.exp(scores - top)
    fresh_expo = jnp.exp(fresh - top)
    total = jnp.sum(expo, axis=2, keepdims=True) + fresh_expo
    weights = (expo / total).astype(BF16)
    fresh_weight = (fresh_expo / total).astype(BF16).astype(F32)
    added = fresh_weight * new_values[...].astype(F32)[:, None, :]
    for r in range(ROWS):
        if r % share == 0:
            copies[PIECES + r // share].wait()
        a_rows[:, r, :] = jnp.dot(weights[r], values[r], preferred_element_type=F32) + added[r]
    for lo in range(Z_LO):
        heads = a_rows[4 * lo : 4 * lo + 4].astype(BF16).reshape(4 * ROWS, HEAD_SIZE)
        for hi in range(Z_HI):
            out[hi * Z_LO + lo, 0 : 4 * ROWS, :] = heads


def project_kernel(place, gathered, weight, out):
    heads = [gathered[:, h * ROWS : (h + 1) * ROWS, :].reshape(EXPERT * ROWS, HEAD_SIZE) for h in range(4)]
    rows = jnp.concatenate(heads, axis=1)
    lo, tp = place[1], place[2]
    extra = gathered[:, 4 * ROWS : 5 * ROWS, :].astype(F32)
    line = lax.broadcasted_iota(jnp.int32, extra.shape, 1)
    resid = jnp.where((line >= tp * 4) & (line < tp * 4 + 4), extra, 0.0).reshape(EXPERT * ROWS, LANES)
    for j in range(TP):
        part = jnp.dot(rows, weight[j], preferred_element_type=F32)
        part = part + jnp.where(lo == j, resid, 0.0)
        part = part.astype(BF16)
        for i in range(Z_LO):
            out[i * TP + j] = part[i * 64 : (i + 1) * 64, :]


def reduce_kernel(parts, out):
    total = parts[0].astype(F32)
    for i in range(1, Z_LO * TP):
        total = total + parts[i].astype(F32)
    total = total.astype(BF16)
    for i in range(EXPERT):
        out[i] = total


def select_kernel(place, gathered, hidden, out, combine):
    tp = place[2]
    mine = place[0] * Z_LO + place[1]
    extra = gathered[:, 4 * ROWS : 5 * ROWS, :].astype(F32)
    line = lax.broadcasted_iota(jnp.int32, extra.shape, 1)
    base = lax.rem(tp + 1, 4) * 4
    route = jnp.sum(jnp.where(line == base, extra, 0.0), axis=1)
    high = jnp.sum(jnp.where(line == base + 1, extra, 0.0), axis=1)
    low = jnp.sum(jnp.where(line == base + 2, extra, 0.0), axis=1)
    pick_row = lax.broadcasted_iota(jnp.int32, (LANES, EXPERT * ROWS), 0) // TOPK
    row = lax.rem(lax.broadcasted_iota(jnp.int32, (LANES, EXPERT * ROWS), 1), ROWS)
    here = jnp.where(pick_row == row, 1.0, 0.0).astype(BF16)
    earlier = jnp.where(pick_row < row, 1.0, 0.0).astype(BF16)
    hits = [jnp.where(route == (a * EXPERT + mine).astype(F32), 1.0, 0.0) for a in range(ATTN)]
    hit = jnp.concatenate(hits, axis=0)
    hit_high = jnp.concatenate([m * high for m in hits], axis=0)
    hit_low = jnp.concatenate([m * low for m in hits], axis=0)
    shape = (ATTN * EXPERT, EXPERT * ROWS)
    own = lax.rem(lax.broadcasted_iota(jnp.int32, shape, 0), EXPERT) == (
        lax.broadcasted_iota(jnp.int32, shape, 1) // ROWS
    )
    dot = lambda a, b: jnp.dot(a.astype(BF16), b, preferred_element_type=F32)
    named = jnp.where(own, dot(hit, here), 0.0)
    rank = dot(hit, earlier)
    weight_high = dot(hit_high, here)
    weight_low = dot(hit_low, here)
    chosen = [jnp.where(rank == s, named, 0.0) for s in (0.0, 1.0)]

    def laid(pair):
        return jnp.concatenate(
            [pair[s][a * EXPERT : (a + 1) * EXPERT, :] for a in range(ATTN) for s in range(2)], axis=0
        )

    choice = laid(chosen).astype(BF16)
    combine[0] = jnp.transpose(laid([c * weight_high for c in chosen])).astype(BF16)
    combine[1] = jnp.transpose(laid([c * weight_low for c in chosen])).astype(BF16)
    for hi in range(Z_HI):
        block = hidden[hi * Z_LO : (hi + 1) * Z_LO].reshape(EXPERT * ROWS, LANES)
        sent = jnp.dot(choice, block, preferred_element_type=F32).astype(BF16)
        sent = sent.reshape(ATTN, SLOTS, LANES)
        for t in range(TP):
            out[:, t, :, hi * LANES : (hi + 1) * LANES] = sent


def expert_kernel(tokens, gain, w_gate, w_up, w_down, out, x, normed):
    slots = ATTN * SLOTS
    square = jnp.zeros((slots, LANES), F32)
    for hi in range(Z_HI):
        for t in range(TP):
            c = hi * TP + t
            block = tokens[:, t, :, hi * LANES : (hi + 1) * LANES].reshape(slots, LANES).astype(F32)
            x[:, c * LANES : (c + 1) * LANES] = block
            square = square + block * block
    factor = lax.rsqrt(jnp.sum(square, axis=1, keepdims=True) * (1.0 / D) + 1e-06)
    normed[...] = (x[...] * factor * gain[...]).astype(BF16)
    gate = jnp.dot(normed[...], w_gate[...], preferred_element_type=F32)
    up = jnp.dot(normed[...], w_up[...], preferred_element_type=F32)
    activated = (gate / (1.0 + jnp.exp(-gate)) * up).astype(BF16)
    for hi in range(Z_HI):
        for t in range(TP):
            c = hi * TP + t
            part = jnp.dot(activated, w_down[:, c * LANES : (c + 1) * LANES], preferred_element_type=F32)
            out[:, t, :, hi * LANES : (hi + 1) * LANES] = part.astype(BF16).reshape(ATTN, SLOTS, LANES)


def combine_kernel(place, parts, combine, hidden, out, total, laid):
    mine = place[0] * Z_LO + place[1]
    row_group = lax.broadcasted_iota(jnp.int32, (EXPERT * ROWS, LANES), 0) // ROWS
    for hi in range(Z_HI):
        columns = slice(hi * LANES, (hi + 1) * LANES)
        block = hidden[hi * Z_LO : (hi + 1) * Z_LO].reshape(EXPERT * ROWS, LANES).astype(F32)
        total[:, columns] = jnp.where(row_group == mine, block, 0.0)
    mixed = total[...]
    for t in range(TP):
        block = parts[:, t].reshape(ATTN * SLOTS, QUARTER)
        mixed = mixed + jnp.dot(combine[0], block, preferred_element_type=F32)
        mixed = mixed + jnp.dot(combine[1], block, preferred_element_type=F32)
    total[...] = mixed
    for n in range(EXPERT * TP):
        for hi in range(Z_HI):
            laid[n, hi * 4 : (hi + 1) * 4, :] = total[n * 4 : (n + 1) * 4, hi * LANES : (hi + 1) * LANES]
    out[...] = laid[...].astype(BF16)


def finish_kernel(parts, out):
    for t in range(TP):
        total = parts[t].astype(F32)
        for e in range(1, EXPERT):
            total = total + parts[e * TP + t].astype(F32)
        for hi in range(Z_HI):
            c = hi * TP + t
            out[:, c * LANES : (c + 1) * LANES] = total[hi * 4 : (hi + 1) * 4, :].astype(BF16)


def exchange(x, axes):
    return lax.all_to_all(x, axes, split_axis=0, concat_axis=0, tiled=True)


def shards(
    query,
    cached_key_store,
    cached_value_store,
    token_keys,
    token_values,
    lengths,
    out_weight,
    resid,
    norm_gain,
    routes,
    route_weight,
    w_gate,
    w_up,
    w_down,
):
    z = ("zhi", "zlo")
    z_hi, z_lo, tp = (lax.axis_index(n) for n in ("zhi", "zlo", "tp"))
    place = jnp.stack([z_hi, z_lo, tp]).astype(jnp.int32)
    weight = exchange(out_weight.reshape(Z_LO, D // Z_LO, LANES), "zlo")
    sent = call(
        attention_kernel,
        [((EXPERT, 5 * ROWS, LANES), BF16)],
        [SMEM, SMEM, VMEM, ANY, ANY] + [VMEM] * 5,
        [
            pltpu.VMEM((ROWS, POSITIONS, HEAD_SIZE), BF16),
            pltpu.VMEM((ROWS, POSITIONS, HEAD_SIZE), BF16),
            pltpu.VMEM((ROWS, HEADS, HEAD_SIZE), F32),
            pltpu.VMEM((HEADS, ROWS, HEAD_SIZE), F32),
            pltpu.VMEM((EXPERT, ROWS, LANES), F32),
            pltpu.SemaphoreType.DMA((2 * PIECES,)),
        ],
        megabytes=16,
    )(
        place, lengths, query, cached_key_store, cached_value_store,
        token_keys, token_values, resid, routes, route_weight,
    )
    sent, weight = lax.optimization_barrier((sent, weight))
    gathered = exchange(sent, z)
    parts = call(project_kernel, [((Z_LO * TP, 64, LANES), BF16)], [SMEM, VMEM, VMEM])(place, gathered, weight)
    parts = exchange(parts, ("zlo", "tp"))
    own = call(reduce_kernel, [((EXPERT, 64, LANES), BF16)], [VMEM])(parts)
    hidden = exchange(own, z)
    outgoing, combine = call(
        select_kernel,
        [((ATTN, TP, SLOTS, QUARTER), BF16), ((2, EXPERT * ROWS, ATTN * SLOTS), BF16)],
        [SMEM, VMEM, VMEM],
    )(place, gathered, hidden)
    incoming = exchange(outgoing.reshape(ATTN * TP, SLOTS, QUARTER), ("attn", "tp"))
    produced = call(
        expert_kernel,
        [((ATTN, TP, SLOTS, QUARTER), BF16)],
        [VMEM] * 5,
        [pltpu.VMEM((ATTN * SLOTS, D), F32), pltpu.VMEM((ATTN * SLOTS, D), BF16)],
    )(incoming.reshape(ATTN, TP, SLOTS, QUARTER), norm_gain.reshape(1, D), w_gate[0], w_up[0], w_down[0])
    returned = exchange(produced.reshape(ATTN * TP, SLOTS, QUARTER), ("attn", "tp"))
    weighted = call(
        combine_kernel,
        [((EXPERT * TP, ROWS, LANES), BF16)],
        [SMEM, VMEM, VMEM, VMEM],
        [pltpu.VMEM((EXPERT * ROWS, QUARTER), F32), pltpu.VMEM((EXPERT * TP, ROWS, LANES), F32)],
    )(place, returned.reshape(ATTN, TP, SLOTS, QUARTER), combine, hidden)
    back = exchange(weighted, (*z, "tp"))
    return call(finish_kernel, [((ROWS // TP, D), BF16)], [VMEM])(back)


def solution(mesh):
    fine = Mesh(mesh.devices.reshape(ATTN, Z_HI, Z_LO, TP), ("attn", "zhi", "zlo", "tp"))
    rows = ("attn", "zhi", "zlo")
    in_specs = (
        P(rows, "tp"),
        P(rows, None, "tp"),
        P(rows, None, "tp"),
        P(rows, "tp"),
        P(rows, "tp"),
        P(rows),
        P("tp", ("zhi", "zlo")),
        P((*rows, "tp"), None),
        P(),
        P(rows, None),
        P(rows, None),
        P(rows, None, "tp"),
        P(rows, None, "tp"),
        P(rows, "tp", None),
    )
    out_specs = P((*rows, "tp"), None)
    return jax.shard_map(shards, mesh=fine, in_specs=in_specs, out_specs=out_specs, check_vma=False)
```

```python
import math

import jax
import jax.numpy as jnp
from jax import lax
from jax.experimental import pallas as pl
from jax.experimental.pallas import tpu as pltpu
from jax.sharding import Mesh
from jax.sharding import PartitionSpec as P

HEADS = 16
HEAD_SIZE = 128
POSITIONS = 128
ROWS = 16
ATTN = 8
Z_HI = 4
Z_LO = 4
EXPERT = Z_HI * Z_LO
TP = 4
D = 2048
LANES = 128
QUARTER = D // TP
CAP = 2
FF = 192
TOPK = 8
PIECES = 4
BF16 = jnp.bfloat16
F32 = jnp.float32

VMEM = pl.BlockSpec(memory_space=pltpu.VMEM)
SMEM = pl.BlockSpec(memory_space=pltpu.SMEM)
ANY = pl.BlockSpec(memory_space=pl.ANY)
PARAMS = pltpu.CompilerParams(vmem_limit_bytes=20 * 1024 * 1024)


def call(kernel, outs, in_specs, scratch=(), megabytes=4):
    shapes = [jax.ShapeDtypeStruct(s, d) for s, d in outs]
    single = len(shapes) == 1
    return pl.pallas_call(
        kernel,
        out_shape=shapes[0] if single else shapes,
        in_specs=in_specs,
        out_specs=VMEM if single else [VMEM] * len(shapes),
        scratch_shapes=list(scratch),
        compiler_params=PARAMS,
        cost_estimate=pl.CostEstimate(flops=0, bytes_accessed=megabytes << 20, transcendentals=0),
    )


def attention_kernel(
    place, lengths, query, keys_hbm, values_hbm, new_keys, new_values, resid, routes, route_weight, out,
    keys, values, q_rows, a_rows, extra, sems,
):
    share = ROWS // PIECES
    copies = []
    for n, (source, target) in enumerate(((keys_hbm, keys), (values_hbm, values))):
        for c in range(PIECES):
            part = pl.ds(c * share, share)
            copies.append(pltpu.make_async_copy(source.at[part], target.at[part], sems.at[n * PIECES + c]))
            copies[-1].start()
    tp = place[2]
    high = route_weight[...].astype(BF16)
    low = (route_weight[...] - high.astype(F32)).astype(BF16)
    pick = lax.rem(lax.broadcasted_iota(jnp.int32, (TOPK, LANES), 1), TOPK)
    spread = jnp.where(pick == lax.broadcasted_iota(jnp.int32, (TOPK, LANES), 0), 1.0, 0.0).astype(BF16)
    diagonal = lax.broadcasted_iota(jnp.int32, (ROWS, LANES), 1) // TOPK == lax.broadcasted_iota(
        jnp.int32, (ROWS, LANES), 0
    )
    extra[...] = jnp.zeros_like(extra)
    for n, table in enumerate((routes[...].astype(F32).astype(BF16), high, low)):
        wide = jnp.dot(table, spread, preferred_element_type=F32)
        line = jnp.sum(jnp.where(diagonal, wide, 0.0), axis=0, keepdims=True)
        for e in range(EXPERT):
            extra[e, pl.ds(lax.rem(tp + 1, 4) * 4 + n, 1), :] = line
    for e in range(EXPERT):
        extra[e, pl.ds(tp * 4, 4), :] = resid[:, e * LANES : (e + 1) * LANES].astype(F32)
    out[:, 4 * ROWS : 5 * ROWS, :] = extra[...].astype(BF16)
    for h in range(HEADS):
        q_rows[:, h, :] = query[:, h * HEAD_SIZE : (h + 1) * HEAD_SIZE].astype(F32)
    scale = 1.0 / math.sqrt(HEAD_SIZE)
    position = lax.broadcasted_iota(jnp.int32, (HEADS, POSITIONS), 1)
    scores = []
    for r in range(ROWS):
        if r % share == 0:
            copies[r // share].wait()
        product = lax.dot_general(
            q_rows[r].astype(BF16), keys[r], (((1,), (1,)), ((), ())), preferred_element_type=F32
        )
        scores.append(jnp.where(position < lengths[r], product * scale, -jnp.inf))
    scores = jnp.stack(scores)
    fresh = jnp.sum(q_rows[...] * new_keys[...].astype(F32)[:, None, :], axis=2, keepdims=True) * scale
    top = jnp.maximum(jnp.max(scores, axis=2, keepdims=True), fresh)
    expo = jnp.exp(scores - top)
    fresh_expo = jnp.exp(fresh - top)
    total = jnp.sum(expo, axis=2, keepdims=True) + fresh_expo
    weights = (expo / total).astype(BF16)
    fresh_weight = (fresh_expo / total).astype(BF16).astype(F32)
    added = fresh_weight * new_values[...].astype(F32)[:, None, :]
    for r in range(ROWS):
        if r % share == 0:
            copies[PIECES + r // share].wait()
        a_rows[:, r, :] = jnp.dot(weights[r], values[r], preferred_element_type=F32) + added[r]
    for lo in range(Z_LO):
        heads = a_rows[4 * lo : 4 * lo + 4].astype(BF16).reshape(4 * ROWS, HEAD_SIZE)
        for hi in range(Z_HI):
            out[hi * Z_LO + lo, 0 : 4 * ROWS, :] = heads


def project_kernel(place, gathered, weight, out):
    heads = [gathered[:, h * ROWS : (h + 1) * ROWS, :].reshape(EXPERT * ROWS, HEAD_SIZE) for h in range(4)]
    rows = jnp.concatenate(heads, axis=1)
    lo, tp = place[1], place[2]
    extra = gathered[:, 4 * ROWS : 5 * ROWS, :].astype(F32)
    line = lax.broadcasted_iota(jnp.int32, extra.shape, 1)
    resid = jnp.where((line >= tp * 4) & (line < tp * 4 + 4), extra, 0.0).reshape(EXPERT * ROWS, LANES)
    for j in range(TP):
        part = jnp.dot(rows, weight[j], preferred_element_type=F32)
        part = part + jnp.where(lo == j, resid, 0.0)
        part = part.astype(BF16)
        for i in range(Z_LO):
            out[i * TP + j] = part[i * 64 : (i + 1) * 64, :]


def reduce_kernel(parts, out):
    total = parts[0].astype(F32)
    for i in range(1, Z_LO * TP):
        total = total + parts[i].astype(F32)
    total = total.astype(BF16)
    for i in range(EXPERT):
        out[i] = total


def routing_kernel(place, gathered, choice, combine):
    tp = place[2]
    mine = place[0] * Z_LO + place[1]
    extra = gathered[:, 4 * ROWS : 5 * ROWS, :].astype(F32)
    line = lax.broadcasted_iota(jnp.int32, extra.shape, 1)
    base = lax.rem(tp + 1, 4) * 4
    route = jnp.sum(jnp.where(line == base, extra, 0.0), axis=1)
    high = jnp.sum(jnp.where(line == base + 1, extra, 0.0), axis=1)
    low = jnp.sum(jnp.where(line == base + 2, extra, 0.0), axis=1)
    pick_row = lax.broadcasted_iota(jnp.int32, (LANES, EXPERT * ROWS), 0) // TOPK
    row = lax.rem(lax.broadcasted_iota(jnp.int32, (LANES, EXPERT * ROWS), 1), ROWS)
    here = jnp.where(pick_row == row, 1.0, 0.0).astype(BF16)
    earlier = jnp.where(pick_row < row, 1.0, 0.0).astype(BF16)
    hits = [jnp.where(route == (a * EXPERT + mine).astype(F32), 1.0, 0.0) for a in range(ATTN)]
    hit = jnp.concatenate(hits, axis=0)
    hit_high = jnp.concatenate([m * high for m in hits], axis=0)
    hit_low = jnp.concatenate([m * low for m in hits], axis=0)
    shape = (ATTN * EXPERT, EXPERT * ROWS)
    own = lax.rem(lax.broadcasted_iota(jnp.int32, shape, 0), EXPERT) == (
        lax.broadcasted_iota(jnp.int32, shape, 1) // ROWS
    )
    dot = lambda a, b: jnp.dot(a.astype(BF16), b, preferred_element_type=F32)
    named = jnp.where(own, dot(hit, here), 0.0)
    rank = dot(hit, earlier)
    weight_high = dot(hit_high, here)
    weight_low = dot(hit_low, here)
    for s in range(CAP):
        chosen = jnp.where(rank == float(s), named, 0.0)
        choice[s] = chosen.astype(BF16)
        combine[s, 0] = jnp.transpose(chosen * weight_high).astype(BF16)
        combine[s, 1] = jnp.transpose(chosen * weight_low).astype(BF16)


def select_kernel(choice, hidden, out):
    for hi in range(Z_HI):
        block = hidden[hi * Z_LO : (hi + 1) * Z_LO].reshape(EXPERT * ROWS, LANES)
        for s in range(CAP):
            sent = jnp.dot(choice[s], block, preferred_element_type=F32).astype(BF16)
            sent = sent.reshape(ATTN, EXPERT, LANES)
            for t in range(s, TP, CAP):
                out[:, t, :, hi * LANES : (hi + 1) * LANES] = sent


def expert_kernel(
    tokens, gain, gate_a, up_a, down_a, gate_b, gate_c, up_b, up_c, down_b, down_c, out, x, normed
):
    slots = ATTN * EXPERT
    square = jnp.zeros((slots, LANES), F32)
    for hi in range(Z_HI):
        for t in range(TP):
            c = hi * TP + t
            block = tokens[:, t, :, hi * LANES : (hi + 1) * LANES].reshape(slots, LANES).astype(F32)
            x[:, c * LANES : (c + 1) * LANES] = block
            square = square + block * block
    factor = lax.rsqrt(jnp.sum(square, axis=1, keepdims=True) * (1.0 / D) + 1e-06)
    normed[...] = (x[...] * factor * gain[...]).astype(BF16)
    rows = normed[...]
    turned = (((1,), (1,)), ((), ()))
    joined = lambda *refs: jnp.concatenate([r[...] for r in refs], axis=0)
    gate = lax.dot_general(rows, joined(gate_a, gate_b, gate_c), turned, preferred_element_type=F32)
    up = lax.dot_general(rows, joined(up_a, up_b, up_c), turned, preferred_element_type=F32)
    activated = (gate / (1.0 + jnp.exp(-gate)) * up).astype(BF16)
    for hi in range(Z_HI):
        columns = slice(hi * QUARTER, (hi + 1) * QUARTER)
        down = jnp.concatenate([r[:, columns] for r in (down_a, down_b, down_c)], axis=0)
        part = jnp.dot(activated, down, preferred_element_type=F32).astype(BF16)
        for t in range(TP):
            block = part[:, t * LANES : (t + 1) * LANES].reshape(ATTN, EXPERT, LANES)
            out[:, t, :, hi * LANES : (hi + 1) * LANES] = block


def combine_kernel(place, parts, combine, hidden, out, total, laid):
    mine = place[0] * Z_LO + place[1]
    row_group = lax.broadcasted_iota(jnp.int32, (EXPERT * ROWS, LANES), 0) // ROWS
    for hi in range(Z_HI):
        columns = slice(hi * LANES, (hi + 1) * LANES)
        block = hidden[hi * Z_LO : (hi + 1) * Z_LO].reshape(EXPERT * ROWS, LANES).astype(F32)
        total[:, columns] = jnp.where(row_group == mine, block, 0.0)
    mixed = total[...]
    for t in range(TP):
        block = parts[:, t].reshape(ATTN * EXPERT, QUARTER)
        mixed = mixed + jnp.dot(combine[t % CAP, 0], block, preferred_element_type=F32)
        mixed = mixed + jnp.dot(combine[t % CAP, 1], block, preferred_element_type=F32)
    total[...] = mixed
    for n in range(EXPERT * TP):
        for hi in range(Z_HI):
            laid[n, hi * 4 : (hi + 1) * 4, :] = total[n * 4 : (n + 1) * 4, hi * LANES : (hi + 1) * LANES]
    out[...] = laid[...].astype(BF16)


def finish_kernel(parts, out):
    for t in range(TP):
        total = parts[t].astype(F32)
        for e in range(1, EXPERT):
            total = total + parts[e * TP + t].astype(F32)
        for hi in range(Z_HI):
            c = hi * TP + t
            out[:, c * LANES : (c + 1) * LANES] = total[hi * 4 : (hi + 1) * 4, :].astype(BF16)


def exchange(x, axes):
    return lax.all_to_all(x, axes, split_axis=0, concat_axis=0, tiled=True)


def shards(
    query,
    cached_key_store,
    cached_value_store,
    token_keys,
    token_values,
    lengths,
    out_weight,
    resid,
    norm_gain,
    routes,
    route_weight,
    w_gate,
    w_up,
    w_down,
):
    z = ("zhi", "zlo")
    z_hi, z_lo, tp = (lax.axis_index(n) for n in ("zhi", "zlo", "tp"))
    place = jnp.stack([z_hi, z_lo, tp]).astype(jnp.int32)
    own_part = (w_gate[0].T, w_up[0].T, w_down[0])
    ring = {d: [(i, (i + d) % TP) for i in range(TP)] for d in (1, -1)}
    taken = [
        (lax.ppermute(w[: FF // 2], "tp", ring[-1]), lax.ppermute(w[FF // 2 :], "tp", ring[1])) for w in own_part
    ]
    weight = exchange(out_weight.reshape(Z_LO, D // Z_LO, LANES), "zlo")
    sent = call(
        attention_kernel,
        [((EXPERT, 5 * ROWS, LANES), BF16)],
        [SMEM, SMEM, VMEM, ANY, ANY] + [VMEM] * 5,
        [
            pltpu.VMEM((ROWS, POSITIONS, HEAD_SIZE), BF16),
            pltpu.VMEM((ROWS, POSITIONS, HEAD_SIZE), BF16),
            pltpu.VMEM((ROWS, HEADS, HEAD_SIZE), F32),
            pltpu.VMEM((HEADS, ROWS, HEAD_SIZE), F32),
            pltpu.VMEM((EXPERT, ROWS, LANES), F32),
            pltpu.SemaphoreType.DMA((2 * PIECES,)),
        ],
        megabytes=16,
    )(
        place, lengths, query, cached_key_store, cached_value_store,
        token_keys, token_values, resid, routes, route_weight,
    )
    sent, weight, gates = lax.optimization_barrier((sent, weight, taken[0]))
    gathered = exchange(sent, z)
    parts = call(project_kernel, [((Z_LO * TP, 64, LANES), BF16)], [SMEM, VMEM, VMEM])(place, gathered, weight)
    parts, ups = lax.optimization_barrier((parts, taken[1]))
    parts = exchange(parts, ("zlo", "tp"))
    own = call(reduce_kernel, [((EXPERT, 64, LANES), BF16)], [VMEM])(parts)
    hidden = exchange(own, z)
    choice, combine = call(
        routing_kernel,
        [
            ((CAP, ATTN * EXPERT, EXPERT * ROWS), BF16),
            ((CAP, 2, EXPERT * ROWS, ATTN * EXPERT), BF16),
        ],
        [SMEM, VMEM],
    )(place, gathered)
    outgoing = call(select_kernel, [((ATTN, TP, EXPERT, QUARTER), BF16)], [VMEM, VMEM])(choice, hidden)
    outgoing, downs = lax.optimization_barrier((outgoing, taken[2]))
    incoming = exchange(outgoing.reshape(ATTN * TP, EXPERT, QUARTER), ("attn", "tp"))
    produced = call(
        expert_kernel,
        [((ATTN, TP, EXPERT, QUARTER), BF16)],
        [VMEM] * 11,
        [pltpu.VMEM((ATTN * EXPERT, D), F32), pltpu.VMEM((ATTN * EXPERT, D), BF16)],
    )(incoming.reshape(ATTN, TP, EXPERT, QUARTER), norm_gain.reshape(1, D), *own_part, *gates, *ups, *downs)
    returned = exchange(produced.reshape(ATTN * TP, EXPERT, QUARTER), ("attn", "tp"))
    weighted = call(
        combine_kernel,
        [((EXPERT * TP, ROWS, LANES), BF16)],
        [SMEM, VMEM, VMEM, VMEM],
        [pltpu.VMEM((EXPERT * ROWS, QUARTER), F32), pltpu.VMEM((EXPERT * TP, ROWS, LANES), F32)],
    )(place, returned.reshape(ATTN, TP, EXPERT, QUARTER), combine, hidden)
    back = exchange(weighted, (*z, "tp"))
    return call(finish_kernel, [((ROWS // TP, D), BF16)], [VMEM])(back)


def solution(mesh):
    fine = Mesh(mesh.devices.reshape(ATTN, Z_HI, Z_LO, TP), ("attn", "zhi", "zlo", "tp"))
    rows = ("attn", "zhi", "zlo")
    in_specs = (
        P(rows, "tp"),
        P(rows, None, "tp"),
        P(rows, None, "tp"),
        P(rows, "tp"),
        P(rows, "tp"),
        P(rows),
        P("tp", ("zhi", "zlo")),
        P((*rows, "tp"), None),
        P(),
        P(rows, None),
        P(rows, None),
        P(rows, None, "tp"),
        P(rows, None, "tp"),
        P(rows, "tp", None),
    )
    out_specs = P((*rows, "tp"), None)
    return jax.shard_map(shards, mesh=fine, in_specs=in_specs, out_specs=out_specs, check_vma=False)
```

```python
import math

import jax
import jax.numpy as jnp
from jax import lax
from jax.experimental import pallas as pl
from jax.experimental.pallas import tpu as pltpu
from jax.sharding import Mesh
from jax.sharding import PartitionSpec as P

HEADS = 16
HEAD_SIZE = 128
POSITIONS = 128
ROWS = 16
ATTN = 8
Z_HI = 8
Z_LO = 2
EXPERT = Z_HI * Z_LO
TP = 4
D = 2048
LANES = 128
QUARTER = D // TP
CHUNKS = 4
BLOCK = 64
SENT_HEADS = HEADS // Z_LO
SENT = SENT_HEADS * ROWS
MORE = 8
CAP = 2
FF = 192
TOPK = 8
PIECES = 4
BF16 = jnp.bfloat16
F32 = jnp.float32

VMEM = pl.BlockSpec(memory_space=pltpu.VMEM)
SMEM = pl.BlockSpec(memory_space=pltpu.SMEM)
ANY = pl.BlockSpec(memory_space=pl.ANY)


def call(kernel, outs, in_specs, scratch=(), megabytes=4, limit=20):
    shapes = [jax.ShapeDtypeStruct(s, d) for s, d in outs]
    single = len(shapes) == 1
    return pl.pallas_call(
        kernel,
        out_shape=shapes[0] if single else shapes,
        in_specs=in_specs,
        out_specs=VMEM if single else [VMEM] * len(shapes),
        scratch_shapes=list(scratch),
        compiler_params=pltpu.CompilerParams(vmem_limit_bytes=limit << 20),
        cost_estimate=pl.CostEstimate(flops=0, bytes_accessed=megabytes << 20, transcendentals=0),
    )


def attention_kernel(
    lengths, query_hbm, keys_hbm, values_hbm, new_keys_hbm, new_values_hbm, resid_hbm, routes_hbm, route_weight_hbm,
    out, query, keys, values, new_keys, new_values, resid, routes, route_weight, q_rows, a_rows, extra, sems,
):
    share = ROWS // PIECES
    copies = []

    def bring(source, target):
        copies.append(pltpu.make_async_copy(source, target, sems.at[len(copies)]))
        copies[-1].start()

    bring(query_hbm, query)
    for source, target in ((keys_hbm, keys), (values_hbm, values)):
        for c in range(PIECES):
            bring(source.at[pl.ds(c * share, share)], target.at[pl.ds(c * share, share)])
    for source, target in (
        (new_keys_hbm, new_keys),
        (new_values_hbm, new_values),
        (routes_hbm, routes),
        (route_weight_hbm, route_weight),
        (resid_hbm, resid),
    ):
        bring(source, target)
    copies[0].wait()
    for h in range(HEADS):
        q_rows[:, h, :] = query[:, h * HEAD_SIZE : (h + 1) * HEAD_SIZE].astype(F32)
    scale = 1.0 / math.sqrt(HEAD_SIZE)
    position = lax.broadcasted_iota(jnp.int32, (HEADS, POSITIONS), 1)
    scores = []
    for r in range(ROWS):
        if r % share == 0:
            copies[1 + r // share].wait()
        product = lax.dot_general(
            q_rows[r].astype(BF16), keys[r], (((1,), (1,)), ((), ())), preferred_element_type=F32
        )
        scores.append(jnp.where(position < lengths[r], product * scale, -jnp.inf))
    scores = jnp.stack(scores)
    for copy in copies[1 + 2 * PIECES :]:
        copy.wait()
    high = route_weight[...].astype(BF16)
    low = (route_weight[...] - high.astype(F32)).astype(BF16)
    pick = lax.rem(lax.broadcasted_iota(jnp.int32, (TOPK, LANES), 1), TOPK)
    spread = jnp.where(pick == lax.broadcasted_iota(jnp.int32, (TOPK, LANES), 0), 1.0, 0.0).astype(BF16)
    diagonal = lax.broadcasted_iota(jnp.int32, (ROWS, LANES), 1) // TOPK == lax.broadcasted_iota(
        jnp.int32, (ROWS, LANES), 0
    )
    lines = [jnp.zeros((1, LANES), F32)]
    for table in (routes[...].astype(F32).astype(BF16), high, low):
        wide = lax.dot_general(table, spread, (((0,), (0,)), ((), ())), preferred_element_type=F32)
        lines.insert(-1, jnp.sum(jnp.where(diagonal, wide, 0.0), axis=0, keepdims=True))
    for e in range(EXPERT):
        extra[e, 0:4, :] = resid[:, e * LANES : (e + 1) * LANES].astype(F32)
        for n, line in enumerate(lines):
            extra[e, 4 + n : 5 + n, :] = line
    out[:, SENT : SENT + MORE, :] = extra[...].astype(BF16)
    fresh = jnp.sum(q_rows[...] * new_keys[...].astype(F32)[:, None, :], axis=2, keepdims=True) * scale
    top = jnp.maximum(jnp.max(scores, axis=2, keepdims=True), fresh)
    expo = jnp.exp(scores - top)
    fresh_expo = jnp.exp(fresh - top)
    total = jnp.sum(expo, axis=2, keepdims=True) + fresh_expo
    weights = (expo / total).astype(BF16)
    fresh_weight = (fresh_expo / total).astype(BF16).astype(F32)
    added = fresh_weight * new_values[...].astype(F32)[:, None, :]
    for r in range(ROWS):
        if r % share == 0:
            copies[1 + PIECES + r // share].wait()
        a_rows[:, r, :] = jnp.dot(weights[r], values[r], preferred_element_type=F32) + added[r]
    for lo in range(Z_LO):
        heads = a_rows[SENT_HEADS * lo : SENT_HEADS * (lo + 1)].astype(BF16).reshape(SENT, HEAD_SIZE)
        for hi in range(Z_HI):
            out[hi * Z_LO + lo, 0:SENT, :] = heads


def project_kernel(gathered, own_weight, other_weight, out):
    heads = [gathered[:, h * ROWS : (h + 1) * ROWS, :].reshape(EXPERT * ROWS, HEAD_SIZE) for h in range(SENT_HEADS)]
    rows = jnp.concatenate(heads, axis=1)
    hi, lo, tp = (lax.axis_index(n) for n in ("zhi", "zlo", "tp"))
    extra = gathered[:, SENT : SENT + MORE, :].astype(F32)
    four = jnp.concatenate([extra[:, 0:4, :]] * 4, axis=1)
    line = lax.broadcasted_iota(jnp.int32, four.shape, 1)
    resid = jnp.where((line >= tp * 4) & (line < tp * 4 + 4), four, 0.0).reshape(EXPERT * ROWS, LANES)
    parts = (
        (lo, jnp.dot(rows, own_weight[lo], preferred_element_type=F32) + resid),
        (1 - lo, jnp.dot(rows, other_weight[...], preferred_element_type=F32)),
    )
    parity = lax.rem(hi, 2)
    for th, part in parts:
        part = part.astype(BF16)
        for h in range(2):
            for i in range(Z_LO):
                first = (h * Z_LO + i) * BLOCK
                out[i, pl.ds(th * 2 + (parity ^ h), 1), :, :] = part[None, first : first + BLOCK, :]


def reduce_kernel(parts, out):
    total = parts[0].astype(F32)
    for i in range(1, Z_LO * TP):
        total = total + parts[i].astype(F32)
    total = total.astype(BF16)
    for i in range(EXPERT):
        out[i] = total


def routing_kernel(gathered, choice, combine):
    mine = lax.axis_index(("zhi", "zlo"))
    extra = gathered[:, SENT : SENT + MORE, :].astype(F32)
    route, high, low = (extra[:, n, :] for n in (4, 5, 6))
    pick_row = lax.broadcasted_iota(jnp.int32, (LANES, EXPERT * ROWS), 0) // TOPK
    row = lax.rem(lax.broadcasted_iota(jnp.int32, (LANES, EXPERT * ROWS), 1), ROWS)
    here = jnp.where(pick_row == row, 1.0, 0.0).astype(BF16)
    earlier = jnp.where(pick_row < row, 1.0, 0.0).astype(BF16)
    hits = [jnp.where(route == (a * EXPERT + mine).astype(F32), 1.0, 0.0) for a in range(ATTN)]
    hit = jnp.concatenate(hits, axis=0)
    hit_high = jnp.concatenate([m * high for m in hits], axis=0)
    hit_low = jnp.concatenate([m * low for m in hits], axis=0)
    shape = (ATTN * EXPERT, EXPERT * ROWS)
    own = lax.rem(lax.broadcasted_iota(jnp.int32, shape, 0), EXPERT) == (
        lax.broadcasted_iota(jnp.int32, shape, 1) // ROWS
    )
    dot = lambda a, b: jnp.dot(a.astype(BF16), b, preferred_element_type=F32)
    named = jnp.where(own, dot(hit, here), 0.0)
    rank = dot(hit, earlier)
    weight_high = dot(hit_high, here)
    weight_low = dot(hit_low, here)
    chosen = [jnp.where(rank == float(s), named, 0.0) for s in range(CAP)]
    for s in range(CAP):
        choice[s] = chosen[s].astype(BF16)
    for n, weight in enumerate((weight_high, weight_low)):
        combine[n] = jnp.transpose(jnp.concatenate([c * weight for c in chosen], axis=0)).astype(BF16)


def select_kernel(choice, hidden, out):
    tl = lax.rem(lax.axis_index("tp"), 2)
    half = EXPERT * ROWS // 2
    groups = EXPERT // 2
    picks = []
    for s in range(CAP):
        whole = choice[s].astype(F32).reshape(ATTN, EXPERT, EXPERT * ROWS)
        for h in range(2):
            pick = whole[:, h * groups : (h + 1) * groups, h * half : (h + 1) * half]
            picks.append(pick.reshape(ATTN * groups, half).astype(BF16))
    for k in range(CHUNKS):
        blocks = [hidden[pl.ds((2 * k + (tl ^ h)) * Z_LO, Z_LO)].reshape(half, LANES) for h in range(2)]
        for s in range(CAP):
            sent = [
                jnp.dot(picks[2 * s + h], blocks[h], preferred_element_type=F32).reshape(ATTN, groups, LANES)
                for h in range(2)
            ]
            sent = jnp.concatenate(sent, axis=1).astype(BF16)
            for t in range(s, TP, CAP):
                out[:, t, :, k * LANES : (k + 1) * LANES] = sent


def expert_kernel(
    tokens, gain, gate_a, up_a, down_a, gate_b, gate_c, up_b, up_c, down_b, down_c, out, x, normed
):
    slots = ATTN * EXPERT
    square = jnp.zeros((slots, LANES), F32)
    early = lax.rem(lax.broadcasted_iota(jnp.int32, (slots, LANES), 0), EXPERT) < EXPERT // 2
    for k in range(CHUNKS):
        pieces = [
            tokens[:, t, :, k * LANES : (k + 1) * LANES].reshape(slots, LANES).astype(F32) for t in range(TP)
        ]
        for p in range(2):
            for th in range(2):
                c = 4 * k + 2 * p + th
                block = jnp.where(early, pieces[2 * th + p], pieces[2 * th + 1 - p])
                x[:, c * LANES : (c + 1) * LANES] = block
                square = square + block * block
    factor = lax.rsqrt(jnp.sum(square, axis=1, keepdims=True) * (1.0 / D) + 1e-06)
    normed[...] = (x[...] * factor * gain[...]).astype(BF16)
    rows = normed[...]
    turned = (((1,), (1,)), ((), ()))
    joined = lambda *refs: jnp.concatenate([r[...] for r in refs], axis=0)
    gate = lax.dot_general(joined(gate_a, gate_b, gate_c), rows, turned, preferred_element_type=F32)
    up = lax.dot_general(joined(up_a, up_b, up_c), rows, turned, preferred_element_type=F32)
    activated = jnp.transpose(gate / (1.0 + jnp.exp(-gate)) * up).astype(BF16)
    for k in range(CHUNKS):
        columns = slice(k * QUARTER, (k + 1) * QUARTER)
        down = jnp.concatenate([r[:, columns] for r in (down_a, down_b, down_c)], axis=0)
        part = jnp.dot(activated, down, preferred_element_type=F32)
        piece = lambda p, th: part[:, (2 * p + th) * LANES : (2 * p + th + 1) * LANES]
        for th in range(2):
            for tl in range(2):
                block = jnp.where(early, piece(tl, th), piece(1 - tl, th)).astype(BF16)
                out[:, 2 * th + tl, :, k * LANES : (k + 1) * LANES] = block.reshape(ATTN, EXPERT, LANES)


def combine_kernel(parts, combine, own, out, total, laid):
    mixed = jnp.zeros((EXPERT * ROWS, QUARTER), F32)
    for t in range(0, TP, CAP):
        block = jnp.concatenate([parts[:, t + s].reshape(ATTN * EXPERT, QUARTER) for s in range(CAP)], axis=0)
        for n in range(2):
            mixed = mixed + jnp.dot(combine[n], block, preferred_element_type=F32)
    for k in range(CHUNKS):
        total[k] = mixed[:, k * LANES : (k + 1) * LANES]
    hi, lo, tp = (lax.axis_index(n) for n in ("zhi", "zlo", "tp"))
    h = lax.rem(tp, 2) ^ lax.rem(hi, 2)
    rows = pl.ds(pl.multiple_of((h * Z_LO + lo) * BLOCK, BLOCK), BLOCK)
    k = lax.div(hi, 2)
    total[k, rows, :] = total[k, rows, :] + own[0].astype(F32)
    for n in range(EXPERT * TP):
        for k in range(CHUNKS):
            laid[n, k * 4 : (k + 1) * 4, :] = total[k, n * 4 : (n + 1) * 4, :]
    out[...] = laid[...].astype(BF16)


def finish_kernel(parts, out):
    totals = []
    for t in range(TP):
        total = parts[t].astype(F32)
        for e in range(1, EXPERT):
            total = total + parts[e * TP + t].astype(F32)
        totals.append(total)
    h = lax.div(lax.axis_index("zhi"), Z_HI // 2)
    for th in range(2):
        for tl in range(2):
            for k in range(CHUNKS):
                c = 4 * k + 2 * (tl ^ h) + th
                columns = pl.ds(pl.multiple_of(c * LANES, LANES), LANES)
                out[:, columns] = totals[2 * th + tl][k * 4 : (k + 1) * 4, :].astype(BF16)


def exchange(x, axes):
    return lax.all_to_all(x, axes, split_axis=0, concat_axis=0, tiled=True)


def shards(
    query,
    cached_key_store,
    cached_value_store,
    token_keys,
    token_values,
    lengths,
    out_weight,
    resid,
    norm_gain,
    routes,
    route_weight,
    w_gate,
    w_up,
    w_down,
):
    z = ("zhi", "zlo")
    z_lo = lax.axis_index("zlo")
    own_part = (w_gate[0].T, w_up[0].T, w_down[0])
    ring = {d: [(i, (i + d) % TP) for i in range(TP)] for d in (1, -1)}
    taken = [
        (lax.ppermute(w[: FF // 2], "tp", ring[-1]), lax.ppermute(w[FF // 2 :], "tp", ring[1])) for w in own_part
    ]
    halves = out_weight.reshape(Z_LO, D // Z_LO, LANES)
    other_weight = lax.ppermute(
        lax.dynamic_index_in_dim(halves, 1 - z_lo, 0, keepdims=False), "zlo", [(0, 1), (1, 0)]
    )
    sent = call(
        attention_kernel,
        [((EXPERT, SENT + MORE, LANES), BF16)],
        [SMEM] + [ANY] * 8,
        [
            pltpu.VMEM((ROWS, HEADS * HEAD_SIZE), BF16),
            pltpu.VMEM((ROWS, POSITIONS, HEAD_SIZE), BF16),
            pltpu.VMEM((ROWS, POSITIONS, HEAD_SIZE), BF16),
            pltpu.VMEM((ROWS, HEAD_SIZE), BF16),
            pltpu.VMEM((ROWS, HEAD_SIZE), BF16),
            pltpu.VMEM((ROWS // TP, D), BF16),
            pltpu.VMEM((TOPK, ROWS), jnp.int32),
            pltpu.VMEM((TOPK, ROWS), F32),
            pltpu.VMEM((ROWS, HEADS, HEAD_SIZE), F32),
            pltpu.VMEM((HEADS, ROWS, HEAD_SIZE), F32),
            pltpu.VMEM((EXPERT, MORE, LANES), F32),
            pltpu.SemaphoreType.DMA((2 * PIECES + 6,)),
        ],
        megabytes=16,
        limit=56,
    )(
        lengths, query, cached_key_store, cached_value_store,
        token_keys, token_values, resid, routes.T, route_weight.T,
    )
    sent, other_weight = lax.optimization_barrier((sent, other_weight))
    gathered = exchange(sent, z)
    parts = call(project_kernel, [((Z_LO, TP, BLOCK, LANES), BF16)], [VMEM] * 3)(
        gathered, halves, other_weight
    )
    parts, ups, gates = lax.optimization_barrier((parts, taken[1], taken[0]))
    parts = exchange(parts.reshape(Z_LO * TP, BLOCK, LANES), ("zlo", "tp"))
    own = call(reduce_kernel, [((EXPERT, BLOCK, LANES), BF16)], [VMEM])(parts)
    hidden = exchange(own, z)
    choice, combine = call(
        routing_kernel,
        [
            ((CAP, ATTN * EXPERT, EXPERT * ROWS), BF16),
            ((2, EXPERT * ROWS, CAP * ATTN * EXPERT), BF16),
        ],
        [VMEM],
    )(gathered)
    outgoing = call(select_kernel, [((ATTN, TP, EXPERT, QUARTER), BF16)], [VMEM, VMEM])(choice, hidden)
    outgoing, downs = lax.optimization_barrier((outgoing, taken[2]))
    incoming = exchange(outgoing.reshape(ATTN * TP, EXPERT, QUARTER), ("attn", "tp"))
    produced = call(
        expert_kernel,
        [((ATTN, TP, EXPERT, QUARTER), BF16)],
        [VMEM] * 11,
        [pltpu.VMEM((ATTN * EXPERT, D), F32), pltpu.VMEM((ATTN * EXPERT, D), BF16)],
    )(incoming.reshape(ATTN, TP, EXPERT, QUARTER), norm_gain.reshape(1, D), *own_part, *gates, *ups, *downs)
    returned = exchange(produced.reshape(ATTN * TP, EXPERT, QUARTER), ("attn", "tp"))
    weighted = call(
        combine_kernel,
        [((EXPERT * TP, ROWS, LANES), BF16)],
        [VMEM, VMEM, VMEM],
        [pltpu.VMEM((CHUNKS, EXPERT * ROWS, LANES), F32), pltpu.VMEM((EXPERT * TP, ROWS, LANES), F32)],
    )(returned.reshape(ATTN, TP, EXPERT, QUARTER), combine, own)
    back = exchange(weighted, (*z, "tp"))
    return call(finish_kernel, [((ROWS // TP, D), BF16)], [VMEM])(back)


def solution(mesh):
    fine = Mesh(mesh.devices.reshape(ATTN, Z_HI, Z_LO, TP), ("attn", "zhi", "zlo", "tp"))
    rows = ("attn", "zhi", "zlo")
    in_specs = (
        P(rows, "tp"),
        P(rows, None, "tp"),
        P(rows, None, "tp"),
        P(rows, "tp"),
        P(rows, "tp"),
        P(rows),
        P("tp", ("zhi", "zlo")),
        P((*rows, "tp"), None),
        P(),
        P(rows, None),
        P(rows, None),
        P(rows, None, "tp"),
        P(rows, None, "tp"),
        P(rows, "tp", None),
    )
    out_specs = P((*rows, "tp"), None)
    return jax.shard_map(shards, mesh=fine, in_specs=in_specs, out_specs=out_specs, check_vma=False)
```

```python
import math

import jax
import jax.numpy as jnp
from jax import lax
from jax.experimental import pallas as pl
from jax.experimental.pallas import tpu as pltpu
from jax.sharding import Mesh
from jax.sharding import PartitionSpec as P

HEADS = 16
HEAD_SIZE = 128
POSITIONS = 128
ROWS = 16
ATTN = 8
Z_HI = 8
Z_LO = 2
EXPERT = Z_HI * Z_LO
TP = 4
D = 2048
LANES = 128
QUARTER = D // TP
CHUNKS = 4
BLOCK = 64
SENT_HEADS = HEADS // Z_LO
SENT = SENT_HEADS * ROWS
MORE = 8
CAP = 2
FF = 192
TOPK = 8
PIECES = 4
BF16 = jnp.bfloat16
F32 = jnp.float32

VMEM = pl.BlockSpec(memory_space=pltpu.VMEM)
SMEM = pl.BlockSpec(memory_space=pltpu.SMEM)
ANY = pl.BlockSpec(memory_space=pl.ANY)


def call(kernel, outs, in_specs, scratch=(), megabytes=4, limit=20):
    shapes = [jax.ShapeDtypeStruct(s, d) for s, d in outs]
    single = len(shapes) == 1
    return pl.pallas_call(
        kernel,
        out_shape=shapes[0] if single else shapes,
        in_specs=in_specs,
        out_specs=VMEM if single else [VMEM] * len(shapes),
        scratch_shapes=list(scratch),
        compiler_params=pltpu.CompilerParams(vmem_limit_bytes=limit << 20),
        cost_estimate=pl.CostEstimate(flops=0, bytes_accessed=megabytes << 20, transcendentals=0),
    )


def attention_kernel(
    lengths, query_hbm, keys_hbm, values_hbm, new_keys_hbm, new_values_hbm, resid_hbm, routes_hbm, route_weight_hbm,
    out, query, keys, values, new_keys, new_values, resid, routes, route_weight, q_rows, a_rows, extra, sems,
):
    share = ROWS // PIECES
    copies = []

    def bring(source, target):
        copies.append(pltpu.make_async_copy(source, target, sems.at[len(copies)]))
        copies[-1].start()

    bring(query_hbm, query)
    for source, target in ((keys_hbm, keys), (values_hbm, values)):
        for c in range(PIECES):
            bring(source.at[pl.ds(c * share, share)], target.at[pl.ds(c * share, share)])
    for source, target in (
        (new_keys_hbm, new_keys),
        (new_values_hbm, new_values),
        (routes_hbm, routes),
        (route_weight_hbm, route_weight),
        (resid_hbm, resid),
    ):
        bring(source, target)
    copies[0].wait()
    for h in range(HEADS):
        q_rows[:, h, :] = query[:, h * HEAD_SIZE : (h + 1) * HEAD_SIZE].astype(F32)
    scale = 1.0 / math.sqrt(HEAD_SIZE)
    position = lax.broadcasted_iota(jnp.int32, (HEADS, POSITIONS), 1)
    scores = []
    for r in range(ROWS):
        if r % share == 0:
            copies[1 + r // share].wait()
        product = lax.dot_general(
            q_rows[r].astype(BF16), keys[r], (((1,), (1,)), ((), ())), preferred_element_type=F32
        )
        scores.append(jnp.where(position < lengths[r], product * scale, -jnp.inf))
    scores = jnp.stack(scores)
    for copy in copies[1 + 2 * PIECES :]:
        copy.wait()
    high = route_weight[...].astype(BF16)
    low = (route_weight[...] - high.astype(F32)).astype(BF16)
    pick = lax.rem(lax.broadcasted_iota(jnp.int32, (TOPK, LANES), 1), TOPK)
    spread = jnp.where(pick == lax.broadcasted_iota(jnp.int32, (TOPK, LANES), 0), 1.0, 0.0).astype(BF16)
    diagonal = lax.broadcasted_iota(jnp.int32, (ROWS, LANES), 1) // TOPK == lax.broadcasted_iota(
        jnp.int32, (ROWS, LANES), 0
    )
    lines = [jnp.zeros((1, LANES), F32)]
    for table in (routes[...].astype(F32).astype(BF16), high, low):
        wide = lax.dot_general(table, spread, (((0,), (0,)), ((), ())), preferred_element_type=F32)
        lines.insert(-1, jnp.sum(jnp.where(diagonal, wide, 0.0), axis=0, keepdims=True))
    for e in range(EXPERT):
        extra[e, 0:4, :] = resid[:, e * LANES : (e + 1) * LANES].astype(F32)
        for n, line in enumerate(lines):
            extra[e, 4 + n : 5 + n, :] = line
    out[:, SENT : SENT + MORE, :] = extra[...].astype(BF16)
    fresh = jnp.sum(q_rows[...] * new_keys[...].astype(F32)[:, None, :], axis=2, keepdims=True) * scale
    top = jnp.maximum(jnp.max(scores, axis=2, keepdims=True), fresh)
    expo = jnp.exp(scores - top)
    fresh_expo = jnp.exp(fresh - top)
    total = jnp.sum(expo, axis=2, keepdims=True) + fresh_expo
    weights = (expo / total).astype(BF16)
    fresh_weight = (fresh_expo / total).astype(BF16).astype(F32)
    added = fresh_weight * new_values[...].astype(F32)[:, None, :]
    for r in range(ROWS):
        if r % share == 0:
            copies[1 + PIECES + r // share].wait()
        a_rows[:, r, :] = jnp.dot(weights[r], values[r], preferred_element_type=F32) + added[r]
    for lo in range(Z_LO):
        heads = a_rows[SENT_HEADS * lo : SENT_HEADS * (lo + 1)].astype(BF16).reshape(SENT, HEAD_SIZE)
        for hi in range(Z_HI):
            out[hi * Z_LO + lo, 0:SENT, :] = heads


def project_kernel(gathered, own_weight, other_weight, out):
    heads = [gathered[:, h * ROWS : (h + 1) * ROWS, :].reshape(EXPERT * ROWS, HEAD_SIZE) for h in range(SENT_HEADS)]
    rows = jnp.concatenate(heads, axis=1)
    hi, lo, tp = (lax.axis_index(n) for n in ("zhi", "zlo", "tp"))
    extra = gathered[:, SENT : SENT + MORE, :].astype(F32)
    four = jnp.concatenate([extra[:, 0:4, :]] * 4, axis=1)
    line = lax.broadcasted_iota(jnp.int32, four.shape, 1)
    resid = jnp.where((line >= tp * 4) & (line < tp * 4 + 4), four, 0.0).reshape(EXPERT * ROWS, LANES)
    parts = (
        (lo, jnp.dot(rows, own_weight[lo], preferred_element_type=F32) + resid),
        (1 - lo, jnp.dot(rows, other_weight[...], preferred_element_type=F32)),
    )
    parity = lax.rem(hi, 2)
    for th, part in parts:
        part = part.astype(BF16)
        for h in range(2):
            for i in range(Z_LO):
                first = (h * Z_LO + i) * BLOCK
                out[i, pl.ds(th * 2 + (parity ^ h), 1), :, :] = part[None, first : first + BLOCK, :]


def reduce_kernel(parts, own, out):
    total = parts[0].astype(F32)
    for i in range(1, Z_LO * TP):
        total = total + parts[i].astype(F32)
    total = total.astype(BF16)
    own[...] = total
    for i in range(EXPERT):
        out[i] = total


def routing_kernel(gathered, tables):
    mine = lax.axis_index(("zhi", "zlo"))
    extra = gathered[:, SENT : SENT + MORE, :].astype(F32)
    route, high, low = (extra[:, n, :] for n in (4, 5, 6))
    pick_row = lax.broadcasted_iota(jnp.int32, (LANES, EXPERT * ROWS), 0) // TOPK
    row = lax.rem(lax.broadcasted_iota(jnp.int32, (LANES, EXPERT * ROWS), 1), ROWS)
    here = jnp.where(pick_row == row, 1.0, 0.0).astype(BF16)
    earlier = jnp.where(pick_row < row, 1.0, 0.0).astype(BF16)
    hits = [jnp.where(route == (a * EXPERT + mine).astype(F32), 1.0, 0.0) for a in range(ATTN)]
    hit = jnp.concatenate(hits, axis=0)
    hit_high = jnp.concatenate([m * high for m in hits], axis=0)
    hit_low = jnp.concatenate([m * low for m in hits], axis=0)
    shape = (ATTN * EXPERT, EXPERT * ROWS)
    own = lax.rem(lax.broadcasted_iota(jnp.int32, shape, 0), EXPERT) == (
        lax.broadcasted_iota(jnp.int32, shape, 1) // ROWS
    )
    dot = lambda a, b: jnp.dot(a.astype(BF16), b, preferred_element_type=F32)
    named = jnp.where(own, dot(hit, here), 0.0)
    rank = dot(hit, earlier)
    weight_high = dot(hit_high, here)
    weight_low = dot(hit_low, here)
    chosen = [jnp.where(rank == float(s), named, 0.0) for s in range(CAP)]
    tables[0] = jnp.concatenate(chosen, axis=0).astype(BF16)
    for n, weight in enumerate((weight_high, weight_low)):
        tables[1 + n] = jnp.transpose(jnp.concatenate([c * weight for c in chosen], axis=0)).astype(BF16)


def select_kernel(tables, hidden, out):
    tl = lax.rem(lax.axis_index("tp"), 2)
    half = EXPERT * ROWS // 2
    groups = EXPERT // 2
    picks = []
    for s in range(CAP):
        whole = tables[0, s * ATTN * EXPERT : (s + 1) * ATTN * EXPERT].astype(F32)
        whole = whole.reshape(ATTN, EXPERT, EXPERT * ROWS)
        for h in range(2):
            pick = whole[:, h * groups : (h + 1) * groups, h * half : (h + 1) * half]
            picks.append(pick.reshape(ATTN * groups, half).astype(BF16))
    for k in range(CHUNKS):
        blocks = [hidden[pl.ds((2 * k + (tl ^ h)) * Z_LO, Z_LO)].reshape(half, LANES) for h in range(2)]
        for s in range(CAP):
            sent = [
                jnp.dot(picks[2 * s + h], blocks[h], preferred_element_type=F32).reshape(ATTN, groups, LANES)
                for h in range(2)
            ]
            sent = jnp.concatenate(sent, axis=1).astype(BF16)
            for t in range(s, TP, CAP):
                out[:, t, :, k * LANES : (k + 1) * LANES] = sent


def expert_kernel(
    tokens, gain, gate_a, up_a, down_a, gate_b, gate_c, up_b, up_c, down_b, down_c, out, x, normed
):
    slots = ATTN * EXPERT
    square = jnp.zeros((slots, LANES), F32)
    early = lax.rem(lax.broadcasted_iota(jnp.int32, (slots, LANES), 0), EXPERT) < EXPERT // 2
    for k in range(CHUNKS):
        pieces = [
            tokens[:, t, :, k * LANES : (k + 1) * LANES].reshape(slots, LANES).astype(F32) for t in range(TP)
        ]
        for p in range(2):
            for th in range(2):
                c = 4 * k + 2 * p + th
                block = jnp.where(early, pieces[2 * th + p], pieces[2 * th + 1 - p])
                x[:, c * LANES : (c + 1) * LANES] = block
                square = square + block * block
    factor = lax.rsqrt(jnp.sum(square, axis=1, keepdims=True) * (1.0 / D) + 1e-06)
    normed[...] = (x[...] * factor * gain[...]).astype(BF16)
    rows = normed[...]
    turned = (((1,), (1,)), ((), ()))
    joined = lambda *refs: jnp.concatenate([r[...] for r in refs], axis=0)
    gate = lax.dot_general(joined(gate_a, gate_b, gate_c), rows, turned, preferred_element_type=F32)
    up = lax.dot_general(joined(up_a, up_b, up_c), rows, turned, preferred_element_type=F32)
    activated = jnp.transpose(gate / (1.0 + jnp.exp(-gate)) * up).astype(BF16)
    for k in range(CHUNKS):
        columns = slice(k * QUARTER, (k + 1) * QUARTER)
        down = jnp.concatenate([r[:, columns] for r in (down_a, down_b, down_c)], axis=0)
        part = jnp.dot(activated, down, preferred_element_type=F32)
        piece = lambda p, th: part[:, (2 * p + th) * LANES : (2 * p + th + 1) * LANES]
        for th in range(2):
            for tl in range(2):
                block = jnp.where(early, piece(tl, th), piece(1 - tl, th)).astype(BF16)
                out[:, 2 * th + tl, :, k * LANES : (k + 1) * LANES] = block.reshape(ATTN, EXPERT, LANES)


def combine_kernel(parts, tables, own, out, total, laid):
    mixed = jnp.zeros((EXPERT * ROWS, QUARTER), F32)
    for t in range(0, TP, CAP):
        block = jnp.concatenate([parts[:, t + s].reshape(ATTN * EXPERT, QUARTER) for s in range(CAP)], axis=0)
        for n in range(2):
            mixed = mixed + jnp.dot(tables[1 + n], block, preferred_element_type=F32)
    for k in range(CHUNKS):
        total[k] = mixed[:, k * LANES : (k + 1) * LANES]
    hi, lo, tp = (lax.axis_index(n) for n in ("zhi", "zlo", "tp"))
    h = lax.rem(tp, 2) ^ lax.rem(hi, 2)
    rows = pl.ds(pl.multiple_of((h * Z_LO + lo) * BLOCK, BLOCK), BLOCK)
    k = lax.div(hi, 2)
    total[k, rows, :] = total[k, rows, :] + own[...].astype(F32)
    for n in range(EXPERT * TP):
        for k in range(CHUNKS):
            laid[n, k * 4 : (k + 1) * 4, :] = total[k, n * 4 : (n + 1) * 4, :]
    out[...] = laid[...].astype(BF16)


def finish_kernel(parts, out):
    totals = []
    for t in range(TP):
        total = parts[t].astype(F32)
        for e in range(1, EXPERT):
            total = total + parts[e * TP + t].astype(F32)
        totals.append(total)
    h = lax.div(lax.axis_index("zhi"), Z_HI // 2)
    for th in range(2):
        for tl in range(2):
            for k in range(CHUNKS):
                c = 4 * k + 2 * (tl ^ h) + th
                columns = pl.ds(pl.multiple_of(c * LANES, LANES), LANES)
                out[:, columns] = totals[2 * th + tl][k * 4 : (k + 1) * 4, :].astype(BF16)


def exchange(x, axes):
    return lax.all_to_all(x, axes, split_axis=0, concat_axis=0, tiled=True)


def shards(
    query,
    cached_key_store,
    cached_value_store,
    token_keys,
    token_values,
    lengths,
    out_weight,
    resid,
    norm_gain,
    routes,
    route_weight,
    w_gate,
    w_up,
    w_down,
):
    z = ("zhi", "zlo")
    own_part = (w_gate[0].T, w_up[0].T, w_down[0])
    ring = {d: [(i, (i + d) % TP) for i in range(TP)] for d in (1, -1)}
    taken = [
        (lax.ppermute(w[: FF // 2], "tp", ring[-1]), lax.ppermute(w[FF // 2 :], "tp", ring[1])) for w in own_part
    ]
    halves = out_weight.reshape(Z_LO, D // Z_LO, LANES)
    other_weight = lax.ppermute(
        lax.dynamic_index_in_dim(halves, 1 - lax.axis_index("zlo"), 0, keepdims=False), "zlo", [(0, 1), (1, 0)]
    )
    sent = call(
        attention_kernel,
        [((EXPERT, SENT + MORE, LANES), BF16)],
        [SMEM] + [ANY] * 8,
        [
            pltpu.VMEM((ROWS, HEADS * HEAD_SIZE), BF16),
            pltpu.VMEM((ROWS, POSITIONS, HEAD_SIZE), BF16),
            pltpu.VMEM((ROWS, POSITIONS, HEAD_SIZE), BF16),
            pltpu.VMEM((ROWS, HEAD_SIZE), BF16),
            pltpu.VMEM((ROWS, HEAD_SIZE), BF16),
            pltpu.VMEM((ROWS // TP, D), BF16),
            pltpu.VMEM((TOPK, ROWS), jnp.int32),
            pltpu.VMEM((TOPK, ROWS), F32),
            pltpu.VMEM((ROWS, HEADS, HEAD_SIZE), F32),
            pltpu.VMEM((HEADS, ROWS, HEAD_SIZE), F32),
            pltpu.VMEM((EXPERT, MORE, LANES), F32),
            pltpu.SemaphoreType.DMA((2 * PIECES + 6,)),
        ],
        megabytes=16,
        limit=56,
    )(
        lengths, query, cached_key_store, cached_value_store,
        token_keys, token_values, resid, routes.T, route_weight.T,
    )
    sent, other_weight = lax.optimization_barrier((sent, other_weight))
    gathered = exchange(sent, z)
    parts = call(project_kernel, [((Z_LO, TP, BLOCK, LANES), BF16)], [VMEM] * 3)(
        gathered, halves, other_weight
    )
    parts, ups, gates = lax.optimization_barrier((parts, taken[1], taken[0]))
    parts = exchange(parts.reshape(Z_LO * TP, BLOCK, LANES), ("zlo", "tp"))
    own, spread = call(reduce_kernel, [((BLOCK, LANES), BF16), ((EXPERT, BLOCK, LANES), BF16)], [VMEM])(parts)
    hidden = exchange(spread, z)
    tables = call(routing_kernel, [((3, EXPERT * ROWS, CAP * ATTN * EXPERT), BF16)], [VMEM])(gathered)
    outgoing = call(select_kernel, [((ATTN, TP, EXPERT, QUARTER), BF16)], [VMEM, VMEM])(tables, hidden)
    outgoing, downs = lax.optimization_barrier((outgoing, taken[2]))
    incoming = exchange(outgoing.reshape(ATTN * TP, EXPERT, QUARTER), ("attn", "tp"))
    produced = call(
        expert_kernel,
        [((ATTN, TP, EXPERT, QUARTER), BF16)],
        [VMEM] * 11,
        [pltpu.VMEM((ATTN * EXPERT, D), F32), pltpu.VMEM((ATTN * EXPERT, D), BF16)],
    )(incoming.reshape(ATTN, TP, EXPERT, QUARTER), norm_gain.reshape(1, D), *own_part, *gates, *ups, *downs)
    returned = exchange(produced.reshape(ATTN * TP, EXPERT, QUARTER), ("attn", "tp"))
    weighted = call(
        combine_kernel,
        [((EXPERT * TP, ROWS, LANES), BF16)],
        [VMEM, VMEM, VMEM],
        [pltpu.VMEM((CHUNKS, EXPERT * ROWS, LANES), F32), pltpu.VMEM((EXPERT * TP, ROWS, LANES), F32)],
    )(returned.reshape(ATTN, TP, EXPERT, QUARTER), tables, own)
    back = exchange(weighted, (*z, "tp"))
    return call(finish_kernel, [((ROWS // TP, D), BF16)], [VMEM])(back)


def solution(mesh):
    fine = Mesh(mesh.devices.reshape(ATTN, Z_HI, Z_LO, TP), ("attn", "zhi", "zlo", "tp"))
    rows = ("attn", "zhi", "zlo")
    in_specs = (
        P(rows, "tp"),
        P(rows, None, "tp"),
        P(rows, None, "tp"),
        P(rows, "tp"),
        P(rows, "tp"),
        P(rows),
        P("tp", ("zhi", "zlo")),
        P((*rows, "tp"), None),
        P(),
        P(rows, None),
        P(rows, None),
        P(rows, None, "tp"),
        P(rows, None, "tp"),
        P(rows, "tp", None),
    )
    out_specs = P((*rows, "tp"), None)
    return jax.shard_map(shards, mesh=fine, in_specs=in_specs, out_specs=out_specs, check_vma=False)
```

```python
import math

import jax
import jax.numpy as jnp
from jax import lax
from jax.experimental import pallas as pl
from jax.experimental.pallas import tpu as pltpu
from jax.sharding import Mesh
from jax.sharding import PartitionSpec as P

HEADS = 16
HEAD_SIZE = 128
POSITIONS = 128
ROWS = 16
ATTN = 8
Z_HI = 8
Z_LO = 2
EXPERT = Z_HI * Z_LO
TP = 4
D = 2048
LANES = 128
QUARTER = D // TP
CHUNKS = 4
BLOCK = 64
SENT_HEADS = HEADS // Z_LO
SENT = SENT_HEADS * ROWS
MORE = 8
CAP = 2
FF = 192
TOPK = 8
PIECES = 4
BF16 = jnp.bfloat16
F32 = jnp.float32

VMEM = pl.BlockSpec(memory_space=pltpu.VMEM)
SMEM = pl.BlockSpec(memory_space=pltpu.SMEM)
ANY = pl.BlockSpec(memory_space=pl.ANY)


def call(kernel, outs, in_specs, scratch=(), megabytes=4, limit=20):
    shapes = [jax.ShapeDtypeStruct(s, d) for s, d in outs]
    single = len(shapes) == 1
    return pl.pallas_call(
        kernel,
        out_shape=shapes[0] if single else shapes,
        in_specs=in_specs,
        out_specs=VMEM if single else [VMEM] * len(shapes),
        scratch_shapes=list(scratch),
        compiler_params=pltpu.CompilerParams(vmem_limit_bytes=limit << 20),
        cost_estimate=pl.CostEstimate(flops=0, bytes_accessed=megabytes << 20, transcendentals=0),
    )


def attention_kernel(
    lengths, query_hbm, keys_hbm, values_hbm, new_keys_hbm, new_values_hbm, resid_hbm, routes_hbm, route_weight_hbm,
    out, query, keys, values, new_keys, new_values, resid, routes, route_weight, q_rows, a_rows, extra, sems,
):
    share = ROWS // PIECES
    copies = []

    def bring(source, target):
        copies.append(pltpu.make_async_copy(source, target, sems.at[len(copies)]))
        copies[-1].start()

    bring(query_hbm, query)
    for source, target in ((keys_hbm, keys), (values_hbm, values)):
        for c in range(PIECES):
            bring(source.at[pl.ds(c * share, share)], target.at[pl.ds(c * share, share)])
    for source, target in (
        (new_keys_hbm, new_keys),
        (new_values_hbm, new_values),
        (routes_hbm, routes),
        (route_weight_hbm, route_weight),
        (resid_hbm, resid),
    ):
        bring(source, target)
    copies[0].wait()
    for h in range(HEADS):
        q_rows[:, h, :] = query[:, h * HEAD_SIZE : (h + 1) * HEAD_SIZE].astype(F32)
    scale = 1.0 / math.sqrt(HEAD_SIZE)
    position = lax.broadcasted_iota(jnp.int32, (HEADS, POSITIONS), 1)
    scores = []
    for r in range(ROWS):
        if r % share == 0:
            copies[1 + r // share].wait()
        product = lax.dot_general(
            q_rows[r].astype(BF16), keys[r], (((1,), (1,)), ((), ())), preferred_element_type=F32
        )
        scores.append(jnp.where(position < lengths[r], product * scale, -jnp.inf))
    scores = jnp.stack(scores)
    for copy in copies[1 + 2 * PIECES :]:
        copy.wait()
    high = route_weight[...].astype(BF16)
    low = (route_weight[...] - high.astype(F32)).astype(BF16)
    pick = lax.rem(lax.broadcasted_iota(jnp.int32, (TOPK, LANES), 1), TOPK)
    spread = jnp.where(pick == lax.broadcasted_iota(jnp.int32, (TOPK, LANES), 0), 1.0, 0.0).astype(BF16)
    diagonal = lax.broadcasted_iota(jnp.int32, (ROWS, LANES), 1) // TOPK == lax.broadcasted_iota(
        jnp.int32, (ROWS, LANES), 0
    )
    lines = [jnp.zeros((1, LANES), F32)]
    for table in (routes[...].astype(F32).astype(BF16), high, low):
        wide = lax.dot_general(table, spread, (((0,), (0,)), ((), ())), preferred_element_type=F32)
        lines.insert(-1, jnp.sum(jnp.where(diagonal, wide, 0.0), axis=0, keepdims=True))
    for e in range(EXPERT):
        extra[e, 0:4, :] = resid[:, e * LANES : (e + 1) * LANES].astype(F32)
        for n, line in enumerate(lines):
            extra[e, 4 + n : 5 + n, :] = line
    out[:, SENT : SENT + MORE, :] = extra[...].astype(BF16)
    fresh = jnp.sum(q_rows[...] * new_keys[...].astype(F32)[:, None, :], axis=2, keepdims=True) * scale
    top = jnp.maximum(jnp.max(scores, axis=2, keepdims=True), fresh)
    expo = jnp.exp(scores - top)
    fresh_expo = jnp.exp(fresh - top)
    total = jnp.sum(expo, axis=2, keepdims=True) + fresh_expo
    weights = (expo / total).astype(BF16)
    fresh_weight = (fresh_expo / total).astype(BF16).astype(F32)
    added = fresh_weight * new_values[...].astype(F32)[:, None, :]
    for r in range(ROWS):
        if r % share == 0:
            copies[1 + PIECES + r // share].wait()
        a_rows[:, r, :] = jnp.dot(weights[r], values[r], preferred_element_type=F32) + added[r]
    for lo in range(Z_LO):
        heads = a_rows[SENT_HEADS * lo : SENT_HEADS * (lo + 1)].astype(BF16).reshape(SENT, HEAD_SIZE)
        for hi in range(Z_HI):
            out[hi * Z_LO + lo, 0:SENT, :] = heads


def project_kernel(gathered, own_weight, own_lines, other_lines, out, lines):
    heads = [gathered[:, h * ROWS : (h + 1) * ROWS, :].reshape(EXPERT * ROWS, HEAD_SIZE) for h in range(SENT_HEADS)]
    rows = jnp.concatenate(heads, axis=1)
    hi, lo, tp = (lax.axis_index(n) for n in ("zhi", "zlo", "tp"))
    extra = gathered[:, SENT : SENT + MORE, :].astype(F32)
    four = jnp.concatenate([extra[:, 0:4, :]] * 4, axis=1)
    line = lax.broadcasted_iota(jnp.int32, four.shape, 1)
    resid = jnp.where((line >= tp * 4) & (line < tp * 4 + 4), four, 0.0).reshape(EXPERT * ROWS, LANES)
    core = lax.rem(lax.axis_index("attn"), 2)
    lines[pl.ds(core, 1)] = own_lines[...][None]
    lines[pl.ds(1 - core, 1)] = other_lines[...][None]
    other_weight = lines[...].reshape(D // Z_LO, LANES)
    parts = (
        (lo, jnp.dot(rows, own_weight[lo], preferred_element_type=F32) + resid),
        (1 - lo, jnp.dot(rows, other_weight, preferred_element_type=F32)),
    )
    parity = lax.rem(hi, 2)
    for th, part in parts:
        part = part.astype(BF16)
        for h in range(2):
            for i in range(Z_LO):
                first = (h * Z_LO + i) * BLOCK
                out[i, pl.ds(th * 2 + (parity ^ h), 1), :, :] = part[None, first : first + BLOCK, :]


def reduce_kernel(parts, own, out):
    total = parts[0].astype(F32)
    for i in range(1, Z_LO * TP):
        total = total + parts[i].astype(F32)
    total = total.astype(BF16)
    own[...] = total
    for i in range(EXPERT):
        out[i] = total


def routing_kernel(gathered, picks, tables):
    mine = lax.axis_index(("zhi", "zlo"))
    extra = gathered[:, SENT : SENT + MORE, :].astype(F32)
    route, high, low = (extra[:, n, :] for n in (4, 5, 6))
    pick_row = lax.broadcasted_iota(jnp.int32, (LANES, EXPERT * ROWS), 0) // TOPK
    row = lax.rem(lax.broadcasted_iota(jnp.int32, (LANES, EXPERT * ROWS), 1), ROWS)
    here = jnp.where(pick_row == row, 1.0, 0.0).astype(BF16)
    earlier = jnp.where(pick_row < row, 1.0, 0.0).astype(BF16)
    hits = [jnp.where(route == (a * EXPERT + mine).astype(F32), 1.0, 0.0) for a in range(ATTN)]
    hit = jnp.concatenate(hits, axis=0)
    hit_high = jnp.concatenate([m * high for m in hits], axis=0)
    hit_low = jnp.concatenate([m * low for m in hits], axis=0)
    shape = (ATTN * EXPERT, EXPERT * ROWS)
    own = lax.rem(lax.broadcasted_iota(jnp.int32, shape, 0), EXPERT) == (
        lax.broadcasted_iota(jnp.int32, shape, 1) // ROWS
    )
    dot = lambda a, b: jnp.dot(a.astype(BF16), b, preferred_element_type=F32)
    named = jnp.where(own, dot(hit, here), 0.0)
    rank = dot(hit, earlier)
    weight_high = dot(hit_high, here)
    weight_low = dot(hit_low, here)
    chosen = [jnp.where(rank == float(s), named, 0.0) for s in range(CAP)]
    half = EXPERT * ROWS // 2
    for s in range(CAP):
        whole = chosen[s].reshape(ATTN, EXPERT, EXPERT * ROWS)
        for h in range(2):
            pick = whole[:, h * (EXPERT // 2) : (h + 1) * (EXPERT // 2), h * half : (h + 1) * half]
            picks[s, h] = pick.reshape(half // 2, half).astype(BF16)
    for n, weight in enumerate((weight_high, weight_low)):
        tables[n] = jnp.transpose(jnp.concatenate([c * weight for c in chosen], axis=0)).astype(BF16)


def select_kernel(picks, hidden, out):
    tl = lax.rem(lax.axis_index("tp"), 2)
    half = EXPERT * ROWS // 2
    groups = EXPERT // 2
    for k in range(CHUNKS):
        blocks = [hidden[pl.ds((2 * k + (tl ^ h)) * Z_LO, Z_LO)].reshape(half, LANES) for h in range(2)]
        for s in range(CAP):
            sent = [
                jnp.dot(picks[s, h], blocks[h], preferred_element_type=F32).reshape(ATTN, groups, LANES)
                for h in range(2)
            ]
            sent = jnp.concatenate(sent, axis=1).astype(BF16)
            for t in range(s, TP, CAP):
                out[:, t, :, k * LANES : (k + 1) * LANES] = sent


def expert_kernel(
    tokens, gain, gate_a, up_a, down_a, gate_b, gate_c, up_b, up_c, down_b, down_c, out, x, normed
):
    slots = ATTN * EXPERT
    square = jnp.zeros((slots, LANES), F32)
    early = lax.rem(lax.broadcasted_iota(jnp.int32, (slots, LANES), 0), EXPERT) < EXPERT // 2
    for k in range(CHUNKS):
        pieces = [
            tokens[:, t, :, k * LANES : (k + 1) * LANES].reshape(slots, LANES).astype(F32) for t in range(TP)
        ]
        for p in range(2):
            for th in range(2):
                c = 4 * k + 2 * p + th
                block = jnp.where(early, pieces[2 * th + p], pieces[2 * th + 1 - p])
                x[:, c * LANES : (c + 1) * LANES] = block
                square = square + block * block
    factor = lax.rsqrt(jnp.sum(square, axis=1, keepdims=True) * (1.0 / D) + 1e-06)
    normed[...] = (x[...] * factor * gain[...]).astype(BF16)
    rows = normed[...]
    turned = (((1,), (1,)), ((), ()))
    joined = lambda *refs: jnp.concatenate([r[...] for r in refs], axis=0)
    gate = lax.dot_general(joined(gate_a, gate_b, gate_c), rows, turned, preferred_element_type=F32)
    up = lax.dot_general(joined(up_a, up_b, up_c), rows, turned, preferred_element_type=F32)
    activated = jnp.transpose(gate / (1.0 + jnp.exp(-gate)) * up).astype(BF16)
    for k in range(CHUNKS):
        columns = slice(k * QUARTER, (k + 1) * QUARTER)
        down = jnp.concatenate([r[:, columns] for r in (down_a, down_b, down_c)], axis=0)
        part = jnp.dot(activated, down, preferred_element_type=F32)
        piece = lambda p, th: part[:, (2 * p + th) * LANES : (2 * p + th + 1) * LANES]
        for th in range(2):
            for tl in range(2):
                block = jnp.where(early, piece(tl, th), piece(1 - tl, th)).astype(BF16)
                out[:, 2 * th + tl, :, k * LANES : (k + 1) * LANES] = block.reshape(ATTN, EXPERT, LANES)


def combine_kernel(parts, tables, own, out, total, laid):
    mixed = jnp.zeros((EXPERT * ROWS, QUARTER), F32)
    for t in range(0, TP, CAP):
        block = jnp.concatenate([parts[:, t + s].reshape(ATTN * EXPERT, QUARTER) for s in range(CAP)], axis=0)
        for n in range(2):
            mixed = mixed + jnp.dot(tables[n], block, preferred_element_type=F32)
    for k in range(CHUNKS):
        total[k] = mixed[:, k * LANES : (k + 1) * LANES]
    hi, lo, tp = (lax.axis_index(n) for n in ("zhi", "zlo", "tp"))
    h = lax.rem(tp, 2) ^ lax.rem(hi, 2)
    rows = pl.ds(pl.multiple_of((h * Z_LO + lo) * BLOCK, BLOCK), BLOCK)
    k = lax.div(hi, 2)
    total[k, rows, :] = total[k, rows, :] + own[...].astype(F32)
    for n in range(EXPERT * TP):
        for k in range(CHUNKS):
            laid[n, k * 4 : (k + 1) * 4, :] = total[k, n * 4 : (n + 1) * 4, :]
    out[...] = laid[...].astype(BF16)


def finish_kernel(parts, out):
    totals = []
    for t in range(TP):
        total = parts[t].astype(F32)
        for e in range(1, EXPERT):
            total = total + parts[e * TP + t].astype(F32)
        totals.append(total)
    h = lax.div(lax.axis_index("zhi"), Z_HI // 2)
    for th in range(2):
        for tl in range(2):
            for k in range(CHUNKS):
                c = 4 * k + 2 * (tl ^ h) + th
                columns = pl.ds(pl.multiple_of(c * LANES, LANES), LANES)
                out[:, columns] = totals[2 * th + tl][k * 4 : (k + 1) * 4, :].astype(BF16)


def exchange(x, axes):
    return lax.all_to_all(x, axes, split_axis=0, concat_axis=0, tiled=True)


def shards(
    query,
    cached_key_store,
    cached_value_store,
    token_keys,
    token_values,
    lengths,
    out_weight,
    resid,
    norm_gain,
    routes,
    route_weight,
    w_gate,
    w_up,
    w_down,
):
    z = ("zhi", "zlo")
    own_part = (w_gate[0].T, w_up[0].T, w_down[0])
    ring = {d: [(i, (i + d) % TP) for i in range(TP)] for d in (1, -1)}
    taken = [
        (lax.ppermute(w[: FF // 2], "tp", ring[-1]), lax.ppermute(w[FF // 2 :], "tp", ring[1])) for w in own_part
    ]
    halves = out_weight.reshape(Z_LO, D // Z_LO, LANES)
    quarters = out_weight.reshape(2 * Z_LO, D // Z_LO // 2, LANES)
    core = lax.rem(lax.axis_index("attn"), 2)
    mine = (1 - lax.axis_index("zlo")) * 2 + core
    own_lines = lax.ppermute(lax.dynamic_index_in_dim(quarters, mine, 0, keepdims=False), "zlo", [(0, 1), (1, 0)])
    sent = call(
        attention_kernel,
        [((EXPERT, SENT + MORE, LANES), BF16)],
        [SMEM] + [ANY] * 8,
        [
            pltpu.VMEM((ROWS, HEADS * HEAD_SIZE), BF16),
            pltpu.VMEM((ROWS, POSITIONS, HEAD_SIZE), BF16),
            pltpu.VMEM((ROWS, POSITIONS, HEAD_SIZE), BF16),
            pltpu.VMEM((ROWS, HEAD_SIZE), BF16),
            pltpu.VMEM((ROWS, HEAD_SIZE), BF16),
            pltpu.VMEM((ROWS // TP, D), BF16),
            pltpu.VMEM((TOPK, ROWS), jnp.int32),
            pltpu.VMEM((TOPK, ROWS), F32),
            pltpu.VMEM((ROWS, HEADS, HEAD_SIZE), F32),
            pltpu.VMEM((HEADS, ROWS, HEAD_SIZE), F32),
            pltpu.VMEM((EXPERT, MORE, LANES), F32),
            pltpu.SemaphoreType.DMA((2 * PIECES + 6,)),
        ],
        megabytes=16,
        limit=56,
    )(
        lengths, query, cached_key_store, cached_value_store,
        token_keys, token_values, resid, routes.T, route_weight.T,
    )
    sent, own_lines = lax.optimization_barrier((sent, own_lines))
    other_lines = lax.ppermute(own_lines, "attn", [(i, i ^ 1) for i in range(ATTN)])
    gathered = exchange(sent, z)
    parts = call(project_kernel, [((Z_LO, TP, BLOCK, LANES), BF16)], [VMEM] * 4, [pltpu.VMEM((2, D // Z_LO // 2, LANES), BF16)])(
        gathered, halves, own_lines, other_lines
    )
    parts, ups, gates = lax.optimization_barrier((parts, taken[1], taken[0]))
    parts = exchange(parts.reshape(Z_LO * TP, BLOCK, LANES), ("zlo", "tp"))
    own, spread = call(reduce_kernel, [((BLOCK, LANES), BF16), ((EXPERT, BLOCK, LANES), BF16)], [VMEM])(parts)
    hidden = exchange(spread, z)
    picks, tables = call(
        routing_kernel,
        [
            ((CAP, 2, ATTN * EXPERT // 2, EXPERT * ROWS // 2), BF16),
            ((2, EXPERT * ROWS, CAP * ATTN * EXPERT), BF16),
        ],
        [VMEM],
    )(gathered)
    outgoing = call(select_kernel, [((ATTN, TP, EXPERT, QUARTER), BF16)], [VMEM, VMEM])(picks, hidden)
    outgoing, downs = lax.optimization_barrier((outgoing, taken[2]))
    incoming = exchange(outgoing.reshape(ATTN * TP, EXPERT, QUARTER), ("attn", "tp"))
    produced = call(
        expert_kernel,
        [((ATTN, TP, EXPERT, QUARTER), BF16)],
        [VMEM] * 11,
        [pltpu.VMEM((ATTN * EXPERT, D), F32), pltpu.VMEM((ATTN * EXPERT, D), BF16)],
    )(incoming.reshape(ATTN, TP, EXPERT, QUARTER), norm_gain.reshape(1, D), *own_part, *gates, *ups, *downs)
    returned = exchange(produced.reshape(ATTN * TP, EXPERT, QUARTER), ("attn", "tp"))
    weighted = call(
        combine_kernel,
        [((EXPERT * TP, ROWS, LANES), BF16)],
        [VMEM, VMEM, VMEM],
        [pltpu.VMEM((CHUNKS, EXPERT * ROWS, LANES), F32), pltpu.VMEM((EXPERT * TP, ROWS, LANES), F32)],
    )(returned.reshape(ATTN, TP, EXPERT, QUARTER), tables, own)
    back = exchange(weighted, (*z, "tp"))
    return call(finish_kernel, [((ROWS // TP, D), BF16)], [VMEM])(back)


def solution(mesh):
    fine = Mesh(mesh.devices.reshape(ATTN, Z_HI, Z_LO, TP), ("attn", "zhi", "zlo", "tp"))
    rows = ("attn", "zhi", "zlo")
    in_specs = (
        P(rows, "tp"),
        P(rows, None, "tp"),
        P(rows, None, "tp"),
        P(rows, "tp"),
        P(rows, "tp"),
        P(rows),
        P("tp", ("zhi", "zlo")),
        P((*rows, "tp"), None),
        P(),
        P(rows, None),
        P(rows, None),
        P(rows, None, "tp"),
        P(rows, None, "tp"),
        P(rows, "tp", None),
    )
    out_specs = P((*rows, "tp"), None)
    return jax.shard_map(shards, mesh=fine, in_specs=in_specs, out_specs=out_specs, check_vma=False)
```

```python
import math

import jax
import jax.numpy as jnp
from jax import lax
from jax.experimental import pallas as pl
from jax.experimental.pallas import tpu as pltpu
from jax.sharding import Mesh
from jax.sharding import PartitionSpec as P

HEADS = 16
HEAD_SIZE = 128
POSITIONS = 128
ROWS = 16
ATTN = 8
Z_HI = 8
Z_LO = 2
EXPERT = Z_HI * Z_LO
TP = 4
D = 2048
LANES = 128
QUARTER = D // TP
CHUNKS = 4
BLOCK = 64
SENT_HEADS = HEADS // Z_LO
SENT = SENT_HEADS * ROWS
SERVED = 8
MORE = 8
CAP = 2
FF = 192
TOPK = 8
PIECES = 4
BF16 = jnp.bfloat16
F32 = jnp.float32

VMEM = pl.BlockSpec(memory_space=pltpu.VMEM)
SMEM = pl.BlockSpec(memory_space=pltpu.SMEM)
ANY = pl.BlockSpec(memory_space=pl.ANY)


def call(kernel, outs, in_specs, scratch=(), megabytes=4, limit=20):
    shapes = [jax.ShapeDtypeStruct(s, d) for s, d in outs]
    single = len(shapes) == 1
    return pl.pallas_call(
        kernel,
        out_shape=shapes[0] if single else shapes,
        in_specs=in_specs,
        out_specs=VMEM if single else [VMEM] * len(shapes),
        scratch_shapes=list(scratch),
        compiler_params=pltpu.CompilerParams(vmem_limit_bytes=limit << 20),
        cost_estimate=pl.CostEstimate(flops=0, bytes_accessed=megabytes << 20, transcendentals=0),
    )


def attention_kernel(
    lengths, query_hbm, keys_hbm, values_hbm, new_keys_hbm, new_values_hbm, resid_hbm, routes_hbm, route_weight_hbm,
    out, query, keys, values, new_keys, new_values, resid, routes, route_weight, q_rows, a_rows, extra, sems,
):
    share = ROWS // PIECES
    copies = []

    def bring(source, target):
        copies.append(pltpu.make_async_copy(source, target, sems.at[len(copies)]))
        copies[-1].start()

    bring(query_hbm, query)
    for source, target in ((keys_hbm, keys), (values_hbm, values)):
        for c in range(PIECES):
            bring(source.at[pl.ds(c * share, share)], target.at[pl.ds(c * share, share)])
    for source, target in (
        (new_keys_hbm, new_keys),
        (new_values_hbm, new_values),
        (routes_hbm, routes),
        (route_weight_hbm, route_weight),
        (resid_hbm, resid),
    ):
        bring(source, target)
    copies[0].wait()
    for h in range(HEADS):
        q_rows[:, h, :] = query[:, h * HEAD_SIZE : (h + 1) * HEAD_SIZE].astype(F32)
    scale = 1.0 / math.sqrt(HEAD_SIZE)
    position = lax.broadcasted_iota(jnp.int32, (HEADS, POSITIONS), 1)
    scores = []
    for r in range(ROWS):
        if r % share == 0:
            copies[1 + r // share].wait()
        product = lax.dot_general(
            q_rows[r].astype(BF16), keys[r], (((1,), (1,)), ((), ())), preferred_element_type=F32
        )
        scores.append(jnp.where(position < lengths[r], product * scale, -jnp.inf))
    scores = jnp.stack(scores)
    for copy in copies[1 + 2 * PIECES :]:
        copy.wait()
    high = route_weight[...].astype(BF16)
    low = (route_weight[...] - high.astype(F32)).astype(BF16)
    pick = lax.rem(lax.broadcasted_iota(jnp.int32, (TOPK, LANES), 1), TOPK)
    spread = jnp.where(pick == lax.broadcasted_iota(jnp.int32, (TOPK, LANES), 0), 1.0, 0.0).astype(BF16)
    diagonal = lax.broadcasted_iota(jnp.int32, (ROWS, LANES), 1) // TOPK == lax.broadcasted_iota(
        jnp.int32, (ROWS, LANES), 0
    )
    lines = [jnp.zeros((1, LANES), F32)]
    for table in (routes[...].astype(F32).astype(BF16), high, low):
        wide = lax.dot_general(table, spread, (((0,), (0,)), ((), ())), preferred_element_type=F32)
        lines.insert(-1, jnp.sum(jnp.where(diagonal, wide, 0.0), axis=0, keepdims=True))
    for e in range(EXPERT):
        extra[e, 0:4, :] = resid[:, e * LANES : (e + 1) * LANES].astype(F32)
        for n, line in enumerate(lines):
            extra[e, 4 + n : 5 + n, :] = line
    out[:, SENT : SENT + MORE, :] = extra[...].astype(BF16)
    fresh = jnp.sum(q_rows[...] * new_keys[...].astype(F32)[:, None, :], axis=2, keepdims=True) * scale
    top = jnp.maximum(jnp.max(scores, axis=2, keepdims=True), fresh)
    expo = jnp.exp(scores - top)
    fresh_expo = jnp.exp(fresh - top)
    total = jnp.sum(expo, axis=2, keepdims=True) + fresh_expo
    weights = (expo / total).astype(BF16)
    fresh_weight = (fresh_expo / total).astype(BF16).astype(F32)
    added = fresh_weight * new_values[...].astype(F32)[:, None, :]
    for r in range(ROWS):
        if r % share == 0:
            copies[1 + PIECES + r // share].wait()
        a_rows[:, r, :] = jnp.dot(weights[r], values[r], preferred_element_type=F32) + added[r]
    for lo in range(Z_LO):
        heads = a_rows[SENT_HEADS * lo : SENT_HEADS * (lo + 1)].astype(BF16).reshape(SENT, HEAD_SIZE)
        for hi in range(Z_HI):
            out[hi * Z_LO + lo, 0:SENT, :] = heads


def project_kernel(gathered, own_weight, own_lines, other_lines, out, lines):
    heads = [gathered[:, h * ROWS : (h + 1) * ROWS, :].reshape(EXPERT * ROWS, HEAD_SIZE) for h in range(SENT_HEADS)]
    rows = jnp.concatenate(heads, axis=1)
    hi, lo, tp = (lax.axis_index(n) for n in ("zhi", "zlo", "tp"))
    extra = gathered[:, SENT : SENT + MORE, :].astype(F32)
    four = jnp.concatenate([extra[:, 0:4, :]] * 4, axis=1)
    line = lax.broadcasted_iota(jnp.int32, four.shape, 1)
    resid = jnp.where((line >= tp * 4) & (line < tp * 4 + 4), four, 0.0).reshape(EXPERT * ROWS, LANES)
    core = lax.rem(lax.axis_index("attn"), 2)
    lines[pl.ds(core, 1)] = own_lines[...][None]
    lines[pl.ds(1 - core, 1)] = other_lines[...][None]
    other_weight = lines[...].reshape(D // Z_LO, LANES)
    parts = (
        (lo, jnp.dot(rows, own_weight[lo], preferred_element_type=F32) + resid),
        (1 - lo, jnp.dot(rows, other_weight, preferred_element_type=F32)),
    )
    parity = lax.rem(hi, 2)
    for th, part in parts:
        part = part.astype(BF16)
        for h in range(2):
            for i in range(Z_LO):
                groups = [part[e * ROWS : (e + 1) * ROWS, :] for e in range(8 * h + i, 8 * h + 8, 2)]
                out[i, pl.ds(th * 2 + (parity ^ h), 1), :, :] = jnp.concatenate(groups, axis=0)[None]


def reduce_kernel(parts, out):
    total = parts[0].astype(F32)
    for i in range(1, Z_LO * TP):
        total = total + parts[i].astype(F32)
    total = total.astype(BF16)
    for i in range(EXPERT):
        out[i] = total


def routing_kernel(gathered, picks, tables):
    hi, lo = lax.axis_index("zhi"), lax.axis_index("zlo")
    dot = lambda a, b: jnp.dot(a.astype(BF16), b, preferred_element_type=F32)
    pick_row = lax.broadcasted_iota(jnp.int32, (LANES, EXPERT * ROWS), 0) // TOPK
    row = lax.rem(lax.broadcasted_iota(jnp.int32, (LANES, EXPERT * ROWS), 1), ROWS)
    here = jnp.where(pick_row == row, 1.0, 0.0).astype(BF16)
    earlier = jnp.where(pick_row < row, 1.0, 0.0).astype(BF16)

    extra = gathered[:, SENT : SENT + MORE, :].astype(F32)
    order = [2 * q + i for i in range(Z_LO) for q in range(SERVED)]
    route = jnp.concatenate([extra[e : e + 1] for e in order], axis=0)[:, 4, :]
    hit = jnp.concatenate(
        [jnp.where(route == (a * EXPERT + hi * Z_LO + lo).astype(F32), 1.0, 0.0) for a in range(ATTN)], axis=0
    )
    shape = (ATTN * EXPERT, EXPERT * ROWS)
    j = lax.rem(lax.broadcasted_iota(jnp.int32, shape, 0), EXPERT)
    u = lax.broadcasted_iota(jnp.int32, shape, 1) // ROWS
    own = 2 * lax.rem(j, 8) + j // 8 == 8 * (u // 8) + 2 * lax.rem(u, 4) + lax.rem(u // 4, 2)
    named = jnp.where(own, dot(hit, here), 0.0)
    rank = dot(hit, earlier)
    for s in range(CAP):
        picks[s] = jnp.where(rank == float(s), named, 0.0).astype(BF16)

    served = [gathered[pl.ds(2 * q + lo, 1), SENT : SENT + MORE, :].astype(F32) for q in range(SERVED)]
    served = jnp.concatenate(served, axis=0)
    route, high, low = (served[:, n, :] for n in (4, 5, 6))
    hits = [
        jnp.where(route == (a * EXPERT + hi * Z_LO + other).astype(F32), 1.0, 0.0)
        for a in range(ATTN)
        for other in range(Z_LO)
    ]
    hit = jnp.concatenate(hits, axis=0)
    hit_high = jnp.concatenate([m * high for m in hits], axis=0)
    hit_low = jnp.concatenate([m * low for m in hits], axis=0)
    shape = (ATTN * Z_LO * SERVED, SERVED * ROWS)
    own = lax.rem(lax.broadcasted_iota(jnp.int32, shape, 0), SERVED) == (
        lax.broadcasted_iota(jnp.int32, shape, 1) // ROWS
    )
    here, earlier = here[:, : SERVED * ROWS], earlier[:, : SERVED * ROWS]
    named = jnp.where(own, dot(hit, here), 0.0)
    rank = dot(hit, earlier)
    chosen = [jnp.where(rank == float(s), named, 0.0) for s in range(CAP)]
    for n, weight in enumerate((dot(hit_high, here), dot(hit_low, here))):
        tables[n] = jnp.transpose(jnp.concatenate([c * weight for c in chosen], axis=0)).astype(BF16)


def select_kernel(picks, hidden, out):
    tl = lax.rem(lax.axis_index("tp"), 2)
    for k in range(CHUNKS):
        rows = [hidden[pl.ds((2 * k + (tl ^ h)) * Z_LO, Z_LO)].reshape(Z_LO * BLOCK, LANES) for h in range(2)]
        rows = jnp.concatenate(rows, axis=0)
        for s in range(CAP):
            sent = jnp.dot(picks[s], rows, preferred_element_type=F32).astype(BF16).reshape(ATTN, EXPERT, LANES)
            for t in range(s, TP, CAP):
                out[:, t, :, k * LANES : (k + 1) * LANES] = sent


def expert_kernel(
    tokens, gain, gate_a, up_a, down_a, gate_b, gate_c, up_b, up_c, down_b, down_c, out, x, normed
):
    slots = ATTN * EXPERT
    square = jnp.zeros((slots, LANES), F32)
    early = lax.rem(lax.broadcasted_iota(jnp.int32, (slots, LANES), 0), SERVED) < SERVED // 2
    for k in range(CHUNKS):
        pieces = [
            tokens[:, t, :, k * LANES : (k + 1) * LANES].reshape(slots, LANES).astype(F32) for t in range(TP)
        ]
        for p in range(2):
            for th in range(2):
                c = 4 * k + 2 * p + th
                block = jnp.where(early, pieces[2 * th + p], pieces[2 * th + 1 - p])
                x[:, c * LANES : (c + 1) * LANES] = block
                square = square + block * block
    factor = lax.rsqrt(jnp.sum(square, axis=1, keepdims=True) * (1.0 / D) + 1e-06)
    normed[...] = (x[...] * factor * gain[...]).astype(BF16)
    rows = normed[...]
    turned = (((1,), (1,)), ((), ()))
    joined = lambda *refs: jnp.concatenate([r[...] for r in refs], axis=0)
    gate = lax.dot_general(joined(gate_a, gate_b, gate_c), rows, turned, preferred_element_type=F32)
    up = lax.dot_general(joined(up_a, up_b, up_c), rows, turned, preferred_element_type=F32)
    activated = jnp.transpose(gate / (1.0 + jnp.exp(-gate)) * up).astype(BF16)
    for k in range(CHUNKS):
        columns = slice(k * QUARTER, (k + 1) * QUARTER)
        down = jnp.concatenate([r[:, columns] for r in (down_a, down_b, down_c)], axis=0)
        part = jnp.dot(activated, down, preferred_element_type=F32)
        piece = lambda p, th: part[:, (2 * p + th) * LANES : (2 * p + th + 1) * LANES]
        for th in range(2):
            for tl in range(2):
                block = jnp.where(early, piece(tl, th), piece(1 - tl, th)).reshape(ATTN, Z_LO, SERVED, LANES)
                out[:, :, 2 * th + tl, :, k * LANES : (k + 1) * LANES] = block.astype(BF16)


def combine_kernel(parts, tables, spread, out, total, laid, own, sem):
    fetch = pltpu.make_async_copy(spread.at[0], own, sem)
    fetch.start()
    mixed = jnp.zeros((SERVED * ROWS, QUARTER), F32)
    for t in range(0, TP, CAP):
        block = [parts[:, :, t + s].astype(F32).reshape(ATTN * Z_LO * SERVED, QUARTER).astype(BF16) for s in range(CAP)]
        block = jnp.concatenate(block, axis=0)
        for n in range(2):
            mixed = mixed + jnp.dot(tables[n], block, preferred_element_type=F32)
    for k in range(CHUNKS):
        total[k] = mixed[:, k * LANES : (k + 1) * LANES]
    hi, tp = lax.axis_index("zhi"), lax.axis_index("tp")
    h = lax.rem(tp, 2) ^ lax.rem(hi, 2)
    rows = pl.ds(pl.multiple_of(h * BLOCK, BLOCK), BLOCK)
    k = lax.div(hi, 2)
    fetch.wait()
    total[k, rows, :] = total[k, rows, :] + own[...].astype(F32)
    for n in range(Z_HI * TP):
        for k in range(CHUNKS):
            laid[n, k * 4 : (k + 1) * 4, :] = total[k, n * 4 : (n + 1) * 4, :]
    out[...] = laid[...].astype(BF16)


def finish_kernel(parts, out):
    totals = []
    for t in range(TP):
        total = parts[t].astype(F32)
        for e in range(1, Z_HI):
            total = total + parts[e * TP + t].astype(F32)
        totals.append(total)
    h = lax.div(lax.axis_index("zhi"), Z_HI // 2)
    for th in range(2):
        for tl in range(2):
            for k in range(CHUNKS):
                c = 4 * k + 2 * (tl ^ h) + th
                columns = pl.ds(pl.multiple_of(c * LANES, LANES), LANES)
                out[:, columns] = totals[2 * th + tl][k * 4 : (k + 1) * 4, :].astype(BF16)


def exchange(x, axes):
    return lax.all_to_all(x, axes, split_axis=0, concat_axis=0, tiled=True)


def shards(
    query,
    cached_key_store,
    cached_value_store,
    token_keys,
    token_values,
    lengths,
    out_weight,
    resid,
    norm_gain,
    routes,
    route_weight,
    w_gate,
    w_up,
    w_down,
):
    z = ("zhi", "zlo")
    own_part = (w_gate[0].T, w_up[0].T, w_down[0])
    ring = {d: [(i, (i + d) % TP) for i in range(TP)] for d in (1, -1)}
    taken = [
        (lax.ppermute(w[: FF // 2], "tp", ring[-1]), lax.ppermute(w[FF // 2 :], "tp", ring[1])) for w in own_part
    ]
    halves = out_weight.reshape(Z_LO, D // Z_LO, LANES)
    quarters = out_weight.reshape(2 * Z_LO, D // Z_LO // 2, LANES)
    core = lax.rem(lax.axis_index("attn"), 2)
    mine = (1 - lax.axis_index("zlo")) * 2 + core
    own_lines = lax.ppermute(lax.dynamic_index_in_dim(quarters, mine, 0, keepdims=False), "zlo", [(0, 1), (1, 0)])
    sent = call(
        attention_kernel,
        [((EXPERT, SENT + MORE, LANES), BF16)],
        [SMEM] + [ANY] * 8,
        [
            pltpu.VMEM((ROWS, HEADS * HEAD_SIZE), BF16),
            pltpu.VMEM((ROWS, POSITIONS, HEAD_SIZE), BF16),
            pltpu.VMEM((ROWS, POSITIONS, HEAD_SIZE), BF16),
            pltpu.VMEM((ROWS, HEAD_SIZE), BF16),
            pltpu.VMEM((ROWS, HEAD_SIZE), BF16),
            pltpu.VMEM((ROWS // TP, D), BF16),
            pltpu.VMEM((TOPK, ROWS), jnp.int32),
            pltpu.VMEM((TOPK, ROWS), F32),
            pltpu.VMEM((ROWS, HEADS, HEAD_SIZE), F32),
            pltpu.VMEM((HEADS, ROWS, HEAD_SIZE), F32),
            pltpu.VMEM((EXPERT, MORE, LANES), F32),
            pltpu.SemaphoreType.DMA((2 * PIECES + 6,)),
        ],
        megabytes=16,
        limit=56,
    )(
        lengths, query, cached_key_store, cached_value_store,
        token_keys, token_values, resid, routes.T, route_weight.T,
    )
    sent, own_lines = lax.optimization_barrier((sent, own_lines))
    other_lines = lax.ppermute(own_lines, "attn", [(i, i ^ 1) for i in range(ATTN)])
    gathered = exchange(sent, z)
    parts = call(project_kernel, [((Z_LO, TP, BLOCK, LANES), BF16)], [VMEM] * 4, [pltpu.VMEM((2, D // Z_LO // 2, LANES), BF16)])(
        gathered, halves, own_lines, other_lines
    )
    parts, ups, gates = lax.optimization_barrier((parts, taken[1], taken[0]))
    parts = exchange(parts.reshape(Z_LO * TP, BLOCK, LANES), ("zlo", "tp"))
    spread = call(reduce_kernel, [((EXPERT, BLOCK, LANES), BF16)], [VMEM])(parts)
    hidden = exchange(spread, z)
    picks, tables = call(
        routing_kernel,
        [
            ((CAP, ATTN * EXPERT, EXPERT * ROWS), BF16),
            ((2, SERVED * ROWS, CAP * ATTN * Z_LO * SERVED), BF16),
        ],
        [VMEM],
    )(gathered)
    outgoing = call(select_kernel, [((ATTN, TP, EXPERT, QUARTER), BF16)], [VMEM, VMEM])(picks, hidden)
    outgoing, downs = lax.optimization_barrier((outgoing, taken[2]))
    incoming = exchange(outgoing.reshape(ATTN * TP, EXPERT, QUARTER), ("attn", "tp"))
    produced = call(
        expert_kernel,
        [((ATTN, Z_LO, TP, SERVED, QUARTER), BF16)],
        [VMEM] * 11,
        [pltpu.VMEM((ATTN * EXPERT, D), F32), pltpu.VMEM((ATTN * EXPERT, D), BF16)],
    )(incoming.reshape(ATTN, TP, EXPERT, QUARTER), norm_gain.reshape(1, D), *own_part, *gates, *ups, *downs)
    returned = exchange(produced.reshape(ATTN * Z_LO * TP, SERVED, QUARTER), ("attn", "zlo", "tp"))
    weighted = call(
        combine_kernel,
        [((Z_HI * TP, ROWS, LANES), BF16)],
        [VMEM, VMEM, ANY],
        [
            pltpu.VMEM((CHUNKS, SERVED * ROWS, LANES), F32),
            pltpu.VMEM((Z_HI * TP, ROWS, LANES), F32),
            pltpu.VMEM((BLOCK, LANES), BF16),
            pltpu.SemaphoreType.DMA,
        ],
    )(returned.reshape(ATTN, Z_LO, TP, SERVED, QUARTER), tables, spread)
    back = exchange(weighted, ("zhi", "tp"))
    return call(finish_kernel, [((ROWS // TP, D), BF16)], [VMEM])(back)


def solution(mesh):
    fine = Mesh(mesh.devices.reshape(ATTN, Z_HI, Z_LO, TP), ("attn", "zhi", "zlo", "tp"))
    rows = ("attn", "zhi", "zlo")
    in_specs = (
        P(rows, "tp"),
        P(rows, None, "tp"),
        P(rows, None, "tp"),
        P(rows, "tp"),
        P(rows, "tp"),
        P(rows),
        P("tp", ("zhi", "zlo")),
        P((*rows, "tp"), None),
        P(),
        P(rows, None),
        P(rows, None),
        P(rows, None, "tp"),
        P(rows, None, "tp"),
        P(rows, "tp", None),
    )
    out_specs = P((*rows, "tp"), None)
    return jax.shard_map(shards, mesh=fine, in_specs=in_specs, out_specs=out_specs, check_vma=False)
```

```python
import math

import jax
import jax.numpy as jnp
from jax import lax
from jax.experimental import pallas as pl
from jax.experimental.pallas import tpu as pltpu
from jax.sharding import Mesh
from jax.sharding import PartitionSpec as P

HEADS = 16
HEAD_SIZE = 128
POSITIONS = 128
ROWS = 16
ATTN = 8
Z_HI = 8
Z_LO = 2
EXPERT = Z_HI * Z_LO
TP = 4
D = 2048
LANES = 128
QUARTER = D // TP
CHUNKS = 4
BLOCK = 64
SENT_HEADS = HEADS // Z_LO
SENT = SENT_HEADS * ROWS
SERVED = 8
MORE = 8
CAP = 2
FF = 192
TOPK = 8
PIECES = 4
BF16 = jnp.bfloat16
F32 = jnp.float32

VMEM = pl.BlockSpec(memory_space=pltpu.VMEM)
SMEM = pl.BlockSpec(memory_space=pltpu.SMEM)
ANY = pl.BlockSpec(memory_space=pl.ANY)


def call(kernel, outs, in_specs, scratch=(), megabytes=4, limit=20):
    shapes = [jax.ShapeDtypeStruct(s, d) for s, d in outs]
    single = len(shapes) == 1
    return pl.pallas_call(
        kernel,
        out_shape=shapes[0] if single else shapes,
        in_specs=in_specs,
        out_specs=VMEM if single else [VMEM] * len(shapes),
        scratch_shapes=list(scratch),
        compiler_params=pltpu.CompilerParams(vmem_limit_bytes=limit << 20),
        cost_estimate=pl.CostEstimate(flops=0, bytes_accessed=megabytes << 20, transcendentals=0),
    )


def attention_kernel(
    lengths, query_hbm, keys_hbm, values_hbm, new_keys_hbm, new_values_hbm, resid_hbm, routes_hbm, route_weight_hbm,
    out, query, keys, values, new_keys, new_values, resid, routes, route_weight, q_rows, a_rows, extra, sems,
):
    share = ROWS // PIECES
    copies = []

    def bring(source, target):
        copies.append(pltpu.make_async_copy(source, target, sems.at[len(copies)]))
        copies[-1].start()

    bring(query_hbm, query)
    for source, target in ((keys_hbm, keys), (values_hbm, values)):
        for c in range(PIECES):
            bring(source.at[pl.ds(c * share, share)], target.at[pl.ds(c * share, share)])
    for source, target in (
        (new_keys_hbm, new_keys),
        (new_values_hbm, new_values),
        (routes_hbm, routes),
        (route_weight_hbm, route_weight),
        (resid_hbm, resid),
    ):
        bring(source, target)
    copies[0].wait()
    for h in range(HEADS):
        q_rows[:, h, :] = query[:, h * HEAD_SIZE : (h + 1) * HEAD_SIZE].astype(F32)
    scale = 1.0 / math.sqrt(HEAD_SIZE)
    position = lax.broadcasted_iota(jnp.int32, (HEADS, POSITIONS), 1)
    scores = []
    for r in range(ROWS):
        if r % share == 0:
            copies[1 + r // share].wait()
        product = lax.dot_general(
            q_rows[r].astype(BF16), keys[r], (((1,), (1,)), ((), ())), preferred_element_type=F32
        )
        scores.append(jnp.where(position < lengths[r], product * scale, -jnp.inf))
    scores = jnp.stack(scores)
    for copy in copies[1 + 2 * PIECES :]:
        copy.wait()
    high = route_weight[...].astype(BF16)
    low = (route_weight[...] - high.astype(F32)).astype(BF16)
    pick = lax.rem(lax.broadcasted_iota(jnp.int32, (TOPK, LANES), 1), TOPK)
    spread = jnp.where(pick == lax.broadcasted_iota(jnp.int32, (TOPK, LANES), 0), 1.0, 0.0).astype(BF16)
    diagonal = lax.broadcasted_iota(jnp.int32, (ROWS, LANES), 1) // TOPK == lax.broadcasted_iota(
        jnp.int32, (ROWS, LANES), 0
    )
    lines = [jnp.zeros((1, LANES), F32)]
    for table in (routes[...].astype(F32).astype(BF16), high, low):
        wide = lax.dot_general(table, spread, (((0,), (0,)), ((), ())), preferred_element_type=F32)
        lines.insert(-1, jnp.sum(jnp.where(diagonal, wide, 0.0), axis=0, keepdims=True))
    for e in range(EXPERT):
        extra[e, 0:4, :] = resid[:, e * LANES : (e + 1) * LANES].astype(F32)
        for n, line in enumerate(lines):
            extra[e, 4 + n : 5 + n, :] = line
    out[:, SENT : SENT + MORE, :] = extra[...].astype(BF16)
    fresh = jnp.sum(q_rows[...] * new_keys[...].astype(F32)[:, None, :], axis=2, keepdims=True) * scale
    top = jnp.maximum(jnp.max(scores, axis=2, keepdims=True), fresh)
    expo = jnp.exp(scores - top)
    fresh_expo = jnp.exp(fresh - top)
    total = jnp.sum(expo, axis=2, keepdims=True) + fresh_expo
    weights = (expo / total).astype(BF16)
    fresh_weight = (fresh_expo / total).astype(BF16).astype(F32)
    added = fresh_weight * new_values[...].astype(F32)[:, None, :]
    for r in range(ROWS):
        if r % share == 0:
            copies[1 + PIECES + r // share].wait()
        a_rows[:, r, :] = jnp.dot(weights[r], values[r], preferred_element_type=F32) + added[r]
    for lo in range(Z_LO):
        heads = a_rows[SENT_HEADS * lo : SENT_HEADS * (lo + 1)].astype(BF16).reshape(SENT, HEAD_SIZE)
        for hi in range(Z_HI):
            out[hi * Z_LO + lo, 0:SENT, :] = heads


def project_kernel(gathered, own_weight, own_lines, other_lines, out, lines):
    heads = [gathered[:, h * ROWS : (h + 1) * ROWS, :].reshape(EXPERT * ROWS, HEAD_SIZE) for h in range(SENT_HEADS)]
    rows = jnp.concatenate(heads, axis=1)
    hi, lo, tp = (lax.axis_index(n) for n in ("zhi", "zlo", "tp"))
    extra = gathered[:, SENT : SENT + MORE, :].astype(F32)
    four = jnp.concatenate([extra[:, 0:4, :]] * 4, axis=1)
    line = lax.broadcasted_iota(jnp.int32, four.shape, 1)
    resid = jnp.where((line >= tp * 4) & (line < tp * 4 + 4), four, 0.0).reshape(EXPERT * ROWS, LANES)
    core = lax.rem(lax.axis_index("attn"), 2)
    lines[pl.ds(core, 1)] = own_lines[...][None]
    lines[pl.ds(1 - core, 1)] = other_lines[...][None]
    other_weight = lines[...].reshape(D // Z_LO, LANES)
    parts = (
        (lo, jnp.dot(rows, own_weight[lo], preferred_element_type=F32) + resid),
        (1 - lo, jnp.dot(rows, other_weight, preferred_element_type=F32)),
    )
    parity = lax.rem(hi, 2)
    for th, part in parts:
        part = part.astype(BF16)
        for h in range(2):
            for i in range(Z_LO):
                groups = [part[e * ROWS : (e + 1) * ROWS, :] for e in range(8 * h + i, 8 * h + 8, 2)]
                out[i, pl.ds(th * 2 + (parity ^ h), 1), :, :] = jnp.concatenate(groups, axis=0)[None]


def reduce_kernel(parts, out):
    total = parts[0].astype(F32)
    for i in range(1, Z_LO * TP):
        total = total + parts[i].astype(F32)
    total = total.astype(BF16)
    for i in range(EXPERT):
        out[i] = total


def routing_kernel(gathered, picks, tables):
    hi, lo = lax.axis_index("zhi"), lax.axis_index("zlo")
    dot = lambda a, b: jnp.dot(a.astype(BF16), b, preferred_element_type=F32)
    pick_row = lax.broadcasted_iota(jnp.int32, (LANES, EXPERT * ROWS), 0) // TOPK
    row = lax.rem(lax.broadcasted_iota(jnp.int32, (LANES, EXPERT * ROWS), 1), ROWS)
    here = jnp.where(pick_row == row, 1.0, 0.0).astype(BF16)
    earlier = jnp.where(pick_row < row, 1.0, 0.0).astype(BF16)

    extra = gathered[:, SENT : SENT + MORE, :].astype(F32)
    order = [2 * q + i for i in range(Z_LO) for q in range(SERVED)]
    route = jnp.concatenate([extra[e : e + 1] for e in order], axis=0)[:, 4, :]
    hit = jnp.concatenate(
        [jnp.where(route == (a * EXPERT + hi * Z_LO + lo).astype(F32), 1.0, 0.0) for a in range(ATTN)], axis=0
    )
    shape = (ATTN * EXPERT, EXPERT * ROWS)
    j = lax.rem(lax.broadcasted_iota(jnp.int32, shape, 0), EXPERT)
    u = lax.broadcasted_iota(jnp.int32, shape, 1) // ROWS
    own = 2 * lax.rem(j, 8) + j // 8 == 8 * (u // 8) + 2 * lax.rem(u, 4) + lax.rem(u // 4, 2)
    named = jnp.where(own, dot(hit, here), 0.0)
    rank = dot(hit, earlier)
    for s in range(CAP):
        picks[s] = jnp.where(rank == float(s), named, 0.0).astype(BF16)

    served = [gathered[pl.ds(2 * q + lo, 1), SENT : SENT + MORE, :].astype(F32) for q in range(SERVED)]
    served = jnp.concatenate(served, axis=0)
    route, high, low = (served[:, n, :] for n in (4, 5, 6))
    hits = [
        jnp.where(route == (a * EXPERT + hi * Z_LO + other).astype(F32), 1.0, 0.0)
        for a in range(ATTN)
        for other in range(Z_LO)
    ]
    hit = jnp.concatenate(hits, axis=0)
    hit_high = jnp.concatenate([m * high for m in hits], axis=0)
    hit_low = jnp.concatenate([m * low for m in hits], axis=0)
    shape = (ATTN * Z_LO * SERVED, SERVED * ROWS)
    own = lax.rem(lax.broadcasted_iota(jnp.int32, shape, 0), SERVED) == (
        lax.broadcasted_iota(jnp.int32, shape, 1) // ROWS
    )
    here, earlier = here[:, : SERVED * ROWS], earlier[:, : SERVED * ROWS]
    named = jnp.where(own, dot(hit, here), 0.0)
    rank = dot(hit, earlier)
    chosen = [jnp.where(rank == float(s), named, 0.0) for s in range(CAP)]
    for n, weight in enumerate((dot(hit_high, here), dot(hit_low, here))):
        tables[n] = jnp.transpose(jnp.concatenate([c * weight for c in chosen], axis=0)).astype(BF16)


def select_kernel(picks, hidden, out):
    tl = lax.rem(lax.axis_index("tp"), 2)
    for k in range(CHUNKS):
        rows = [hidden[pl.ds((2 * k + (tl ^ h)) * Z_LO, Z_LO)].reshape(Z_LO * BLOCK, LANES) for h in range(2)]
        rows = jnp.concatenate(rows, axis=0)
        for s in range(CAP):
            sent = jnp.dot(picks[s], rows, preferred_element_type=F32).astype(BF16).reshape(ATTN, EXPERT, LANES)
            for t in range(s, TP, CAP):
                out[:, t, :, k * LANES : (k + 1) * LANES] = sent


def expert_kernel(
    tokens, gain, gate_a, up_a, down_a, gate_b, gate_c, up_b, up_c, down_b, down_c, out, x, normed
):
    slots = ATTN * EXPERT
    square = jnp.zeros((slots, LANES), F32)
    early = lax.rem(lax.broadcasted_iota(jnp.int32, (slots, LANES), 0), SERVED) < SERVED // 2
    for k in range(CHUNKS):
        pieces = [
            tokens[:, t, :, k * LANES : (k + 1) * LANES].reshape(slots, LANES).astype(F32) for t in range(TP)
        ]
        for p in range(2):
            for th in range(2):
                c = 4 * k + 2 * p + th
                block = jnp.where(early, pieces[2 * th + p], pieces[2 * th + 1 - p])
                x[:, c * LANES : (c + 1) * LANES] = block
                square = square + block * block
    factor = lax.rsqrt(jnp.sum(square, axis=1, keepdims=True) * (1.0 / D) + 1e-06)
    normed[...] = (x[...] * factor * gain[...]).astype(BF16)
    rows = normed[...]
    turned = (((1,), (1,)), ((), ()))
    joined = lambda *refs: jnp.concatenate([r[...] for r in refs], axis=0)
    gate = lax.dot_general(joined(gate_a, gate_b, gate_c), rows, turned, preferred_element_type=F32)
    up = lax.dot_general(joined(up_a, up_b, up_c), rows, turned, preferred_element_type=F32)
    activated = jnp.transpose(gate / (1.0 + jnp.exp(-gate)) * up).astype(BF16)
    for k in range(CHUNKS):
        columns = slice(k * QUARTER, (k + 1) * QUARTER)
        down = jnp.concatenate([r[:, columns] for r in (down_a, down_b, down_c)], axis=0)
        part = jnp.dot(activated, down, preferred_element_type=F32)
        piece = lambda p, th: part[:, (2 * p + th) * LANES : (2 * p + th + 1) * LANES]
        for th in range(2):
            for tl in range(2):
                block = jnp.where(early, piece(tl, th), piece(1 - tl, th)).reshape(ATTN, Z_LO, SERVED, LANES)
                out[:, :, 2 * th + tl, :, k * LANES : (k + 1) * LANES] = block.astype(BF16)


def combine_kernel(parts, tables, spread, out, total, laid, own, sem):
    fetch = pltpu.make_async_copy(spread.at[0], own, sem)
    fetch.start()
    mixed = jnp.zeros((SERVED * ROWS, QUARTER), F32)
    for t in range(0, TP, CAP):
        block = [parts[:, :, t + s].astype(F32).reshape(ATTN * Z_LO * SERVED, QUARTER).astype(BF16) for s in range(CAP)]
        block = jnp.concatenate(block, axis=0)
        for n in range(2):
            mixed = mixed + jnp.dot(tables[n], block, preferred_element_type=F32)
    for k in range(CHUNKS):
        total[k] = mixed[:, k * LANES : (k + 1) * LANES]
    hi, tp = lax.axis_index("zhi"), lax.axis_index("tp")
    h = lax.rem(tp, 2) ^ lax.rem(hi, 2)
    rows = pl.ds(pl.multiple_of(h * BLOCK, BLOCK), BLOCK)
    k = lax.div(hi, 2)
    fetch.wait()
    total[k, rows, :] = total[k, rows, :] + own[...].astype(F32)
    for n in range(Z_HI * TP):
        for k in range(CHUNKS):
            laid[n, k * 4 : (k + 1) * 4, :] = total[k, n * 4 : (n + 1) * 4, :]
    out[...] = laid[...].astype(BF16)


def finish_kernel(parts, out):
    totals = []
    for t in range(TP):
        total = parts[t].astype(F32)
        for e in range(1, Z_HI):
            total = total + parts[e * TP + t].astype(F32)
        totals.append(total)
    h = lax.div(lax.axis_index("zhi"), Z_HI // 2)
    for th in range(2):
        for tl in range(2):
            for k in range(CHUNKS):
                c = 4 * k + 2 * (tl ^ h) + th
                columns = pl.ds(pl.multiple_of(c * LANES, LANES), LANES)
                out[:, columns] = totals[2 * th + tl][k * 4 : (k + 1) * 4, :].astype(BF16)


def exchange(x, axes):
    return lax.all_to_all(x, axes, split_axis=0, concat_axis=0, tiled=True)


def shards(
    query,
    cached_key_store,
    cached_value_store,
    token_keys,
    token_values,
    lengths,
    out_weight,
    resid,
    norm_gain,
    routes,
    route_weight,
    w_gate,
    w_up,
    w_down,
):
    z = ("zhi", "zlo")
    own_part = (w_gate[0].T, w_up[0].T, w_down[0])
    ring = {d: [(i, (i + d) % TP) for i in range(TP)] for d in (1, -1)}
    halves_of = lambda w: (w[: FF // 2], w[FF // 2 :])
    take = lambda pair: (lax.ppermute(pair[0], "tp", ring[-1]), lax.ppermute(pair[1], "tp", ring[1]))
    gates, ups = take(halves_of(own_part[0])), take(halves_of(own_part[1]))
    halves = out_weight.reshape(Z_LO, D // Z_LO, LANES)
    quarters = out_weight.reshape(2 * Z_LO, D // Z_LO // 2, LANES)
    core = lax.rem(lax.axis_index("attn"), 2)
    mine = (1 - lax.axis_index("zlo")) * 2 + core
    own_lines = lax.ppermute(lax.dynamic_index_in_dim(quarters, mine, 0, keepdims=False), "zlo", [(0, 1), (1, 0)])
    sent = call(
        attention_kernel,
        [((EXPERT, SENT + MORE, LANES), BF16)],
        [SMEM] + [ANY] * 8,
        [
            pltpu.VMEM((ROWS, HEADS * HEAD_SIZE), BF16),
            pltpu.VMEM((ROWS, POSITIONS, HEAD_SIZE), BF16),
            pltpu.VMEM((ROWS, POSITIONS, HEAD_SIZE), BF16),
            pltpu.VMEM((ROWS, HEAD_SIZE), BF16),
            pltpu.VMEM((ROWS, HEAD_SIZE), BF16),
            pltpu.VMEM((ROWS // TP, D), BF16),
            pltpu.VMEM((TOPK, ROWS), jnp.int32),
            pltpu.VMEM((TOPK, ROWS), F32),
            pltpu.VMEM((ROWS, HEADS, HEAD_SIZE), F32),
            pltpu.VMEM((HEADS, ROWS, HEAD_SIZE), F32),
            pltpu.VMEM((EXPERT, MORE, LANES), F32),
            pltpu.SemaphoreType.DMA((2 * PIECES + 6,)),
        ],
        megabytes=16,
        limit=56,
    )(
        lengths, query, cached_key_store, cached_value_store,
        token_keys, token_values, resid, routes.T, route_weight.T,
    )
    sent, own_lines = lax.optimization_barrier((sent, own_lines))
    other_lines = lax.ppermute(own_lines, "attn", [(i, i ^ 1) for i in range(ATTN)])
    gathered = exchange(sent, z)
    parts = call(project_kernel, [((Z_LO, TP, BLOCK, LANES), BF16)], [VMEM] * 4, [pltpu.VMEM((2, D // Z_LO // 2, LANES), BF16)])(
        gathered, halves, own_lines, other_lines
    )
    parts, ups, gates, down_halves = lax.optimization_barrier((parts, ups, gates, halves_of(own_part[2])))
    parts = exchange(parts.reshape(Z_LO * TP, BLOCK, LANES), ("zlo", "tp"))
    spread = call(reduce_kernel, [((EXPERT, BLOCK, LANES), BF16)], [VMEM])(parts)
    hidden = exchange(spread, z)
    picks, tables = call(
        routing_kernel,
        [
            ((CAP, ATTN * EXPERT, EXPERT * ROWS), BF16),
            ((2, SERVED * ROWS, CAP * ATTN * Z_LO * SERVED), BF16),
        ],
        [VMEM],
    )(gathered)
    outgoing = call(select_kernel, [((ATTN, TP, EXPERT, QUARTER), BF16)], [VMEM, VMEM])(picks, hidden)
    outgoing, downs = lax.optimization_barrier((outgoing, take(down_halves)))
    incoming = exchange(outgoing.reshape(ATTN * TP, EXPERT, QUARTER), ("attn", "tp"))
    produced = call(
        expert_kernel,
        [((ATTN, Z_LO, TP, SERVED, QUARTER), BF16)],
        [VMEM] * 11,
        [pltpu.VMEM((ATTN * EXPERT, D), F32), pltpu.VMEM((ATTN * EXPERT, D), BF16)],
    )(incoming.reshape(ATTN, TP, EXPERT, QUARTER), norm_gain.reshape(1, D), *own_part, *gates, *ups, *downs)
    returned = exchange(produced.reshape(ATTN * Z_LO * TP, SERVED, QUARTER), ("attn", "zlo", "tp"))
    weighted = call(
        combine_kernel,
        [((Z_HI * TP, ROWS, LANES), BF16)],
        [VMEM, VMEM, ANY],
        [
            pltpu.VMEM((CHUNKS, SERVED * ROWS, LANES), F32),
            pltpu.VMEM((Z_HI * TP, ROWS, LANES), F32),
            pltpu.VMEM((BLOCK, LANES), BF16),
            pltpu.SemaphoreType.DMA,
        ],
    )(returned.reshape(ATTN, Z_LO, TP, SERVED, QUARTER), tables, spread)
    back = exchange(weighted, ("zhi", "tp"))
    return call(finish_kernel, [((ROWS // TP, D), BF16)], [VMEM])(back)


def solution(mesh):
    fine = Mesh(mesh.devices.reshape(ATTN, Z_HI, Z_LO, TP), ("attn", "zhi", "zlo", "tp"))
    rows = ("attn", "zhi", "zlo")
    in_specs = (
        P(rows, "tp"),
        P(rows, None, "tp"),
        P(rows, None, "tp"),
        P(rows, "tp"),
        P(rows, "tp"),
        P(rows),
        P("tp", ("zhi", "zlo")),
        P((*rows, "tp"), None),
        P(),
        P(rows, None),
        P(rows, None),
        P(rows, None, "tp"),
        P(rows, None, "tp"),
        P(rows, "tp", None),
    )
    out_specs = P((*rows, "tp"), None)
    return jax.shard_map(shards, mesh=fine, in_specs=in_specs, out_specs=out_specs, check_vma=False)
```
